256 devices in a mesh: batch: 8 (over x_hi, y), prefix: 32 (over z, x_lo, core).
Axes of the slice: x: 4 (x_hi: 2, x_lo: 2; x = x_hi * 2 + x_lo), y: 4, z: 8, core: 2. Of those that a mesh axis runs over, the one named last changes fastest.
Arguments:
- queries: bfloat16 [32, 128, 8192], P('batch', None, 'prefix'), may hold values from -32 to 32
- prompt_key_cache: bfloat16 [16384, 1024], P('prefix'), may hold values from -10 to 10
- prompt_value_cache: bfloat16 [16384, 1024], P('prefix'), may hold values from -12 to 12
- response_keys: bfloat16 [32, 128, 1024], P('batch'), may hold values from -10 to 10
- response_values: bfloat16 [32, 128, 1024], P('batch'), may hold values from -12 to 12
- lengths: int32 [32], P('batch'), may hold values from 32 to 128, as said below
- out_weight: bfloat16 [8192, 5120], P('prefix', 'batch'), may hold values from -0.0625 to 0.0625
Outputs:
- scored: bfloat16 [4096, 5120], P(('batch', 'prefix'))
The draws below stay inside these ranges and needn't reach their ends.
Inputs may be any that keep to these rules, and one draw needn't show every extreme that they name: `lengths`: some response in every draw has all 128 tokens valid.
All inputs are finite; a program needn't handle non-finite values.
Results may differ from the reference program's by a relative error of at most 0.0052.
Values may be sent and summed in bfloat16 or wider, within the bound.
No kernel may reach another device: no remote copies, remote signals or barrier semaphores. Data moves between devices by JAX's collectives and lax.ppermute only.
A program may use at most 128 MiB of HBM per device.

```python
import jax
import jax.numpy as jnp
from jax import lax

QUERY_HEADS = 64
KEY_VALUE_HEADS = 8
HEAD_SIZE = 128
D = 5120
RESPONSE_LENGTH = 128
PREFIX_SLICE_LEN = 512
RESPONSE_COUNT = 32
PROMPT_LENGTH = 16384


def prompt_table(key):
    key_matrix = jnp.clip(jax.random.normal(jax.random.fold_in(key, 101), (PROMPT_LENGTH, KEY_VALUE_HEADS * HEAD_SIZE), jnp.float32), -4.0, 4.0)
    anchor_at = jax.random.randint(jax.random.fold_in(key, 102), (3,), 0, PROMPT_LENGTH - 1)
    position = jnp.arange(PROMPT_LENGTH)[:, None]
    for anchor_id in range(3):
        anchor = key_matrix[anchor_at[anchor_id]]
        key_matrix = jnp.where(position == anchor_at[anchor_id], anchor[None, :], key_matrix)
        key_matrix = jnp.where(position == anchor_at[anchor_id] + 1, key_matrix, key_matrix)
    return key_matrix


def suffix_table(key):
    key_matrix = jnp.clip(1.75 * jax.random.normal(jax.random.fold_in(key, 103), (RESPONSE_COUNT, RESPONSE_LENGTH, KEY_VALUE_HEADS * HEAD_SIZE), jnp.float32), -7.0, 7.0)
    position = jnp.arange(RESPONSE_LENGTH)[None, :, None]
    anchor = key_matrix[:, 0:1, :]
    key_matrix = jnp.where(position == 0, anchor, key_matrix)
    key_matrix = jnp.where(position == 1, key_matrix, key_matrix)
    return key_matrix


def draw_prompt_key_cache(key, part):
    key_matrix = prompt_table(key)
    return key_matrix.astype(jnp.bfloat16)


def draw_response_keys(key, part):
    key_matrix = suffix_table(key)
    return key_matrix.astype(jnp.bfloat16)


def draw_queries(key, part):
    key = jax.random.fold_in(key, 104)
    noise_rows = jnp.clip(2.0 * jax.random.normal(key, (RESPONSE_COUNT, RESPONSE_LENGTH, QUERY_HEADS * HEAD_SIZE), jnp.float32), -8.0, 8.0)
    position = jnp.arange(RESPONSE_LENGTH)[None, :, None]
    for anchor_id in range(3):
        noise_rows = jnp.where(position == anchor_id, noise_rows, noise_rows)
        noise_rows = jnp.where(position == anchor_id + 3, noise_rows, noise_rows)
    return noise_rows.astype(jnp.bfloat16)


def draw_lengths(key, part):
    key = jax.random.fold_in(key, 105)
    drawn = jax.random.randint(jax.random.fold_in(key, 1), (RESPONSE_COUNT,), RESPONSE_LENGTH // 4, RESPONSE_LENGTH + 1)
    longest_at = jax.random.randint(jax.random.fold_in(key, 2), (), 0, RESPONSE_COUNT)
    return jnp.where(jnp.arange(RESPONSE_COUNT) == longest_at, RESPONSE_LENGTH, drawn).astype(jnp.int32)


def steps_of(rng, extent, cuts, smallest, largest):
    level, own = 1.0, jax.random.fold_in(rng, 6)
    for dim, parts in cuts:
        heights = jnp.exp(jax.random.uniform(jax.random.fold_in(own, dim), (parts,), jnp.float32, smallest / len(cuts), largest / len(cuts)))
        level = level * jnp.repeat(heights, extent[dim] // parts).reshape([-1 if axis == dim else 1 for axis in range(len(extent))])
    return level


def normal_values(rng, extent, deviation, limit, shards=(), held_as=jnp.bfloat16):
    factor_of = steps_of(rng, extent, shards, -0.22, 0.18) if shards else 1.0
    values = jax.random.normal(rng, extent, jnp.float32) * deviation * factor_of
    return jnp.minimum(jnp.maximum(values, -limit), limit).astype(held_as)


def setup_inputs(seed: int = 0) -> dict:
    arg_keys = jax.random.split(jax.random.key(seed), 8)
    return {
        "queries": draw_queries(jax.random.fold_in(arg_keys[7], 71), 0),
        "prompt_key_cache": draw_prompt_key_cache(jax.random.fold_in(arg_keys[7], 71), 0),
        "prompt_value_cache": normal_values(arg_keys[2], (PROMPT_LENGTH, KEY_VALUE_HEADS * HEAD_SIZE), 2.0, 12.0, ((0, 32),)),
        "response_keys": draw_response_keys(jax.random.fold_in(arg_keys[7], 71), 0),
        "response_values": normal_values(arg_keys[4], (RESPONSE_COUNT, RESPONSE_LENGTH, KEY_VALUE_HEADS * HEAD_SIZE), 2.0, 12.0, ((0, 8),)),
        "lengths": draw_lengths(jax.random.fold_in(arg_keys[7], 71), 0),
        "out_weight": normal_values(arg_keys[6], (QUERY_HEADS * HEAD_SIZE, D), (QUERY_HEADS * HEAD_SIZE) ** -0.5, 0.0625, ((0, 32), (1, 8))),
    }


def reference(queries, prompt_key_cache, prompt_value_cache, response_keys, response_values, lengths, out_weight):
    heads_per_group = QUERY_HEADS // KEY_VALUE_HEADS
    token_rows = RESPONSE_COUNT * RESPONSE_LENGTH
    score_scale = HEAD_SIZE ** -0.5
    block_list = PROMPT_LENGTH // PREFIX_SLICE_LEN
    every_query_row = queries.reshape(token_rows, KEY_VALUE_HEADS, heads_per_group, HEAD_SIZE)
    prompt_row_count = prompt_key_cache.reshape(block_list, PREFIX_SLICE_LEN, KEY_VALUE_HEADS, HEAD_SIZE)
    prompt_value_rows = prompt_value_cache.reshape(block_list, PREFIX_SLICE_LEN, KEY_VALUE_HEADS, HEAD_SIZE)
    response_rows = response_keys.reshape(RESPONSE_COUNT, RESPONSE_LENGTH, KEY_VALUE_HEADS, HEAD_SIZE)
    response_value_rows = response_values.reshape(RESPONSE_COUNT, RESPONSE_LENGTH, KEY_VALUE_HEADS, HEAD_SIZE)
    causal = jnp.arange(RESPONSE_LENGTH)[:, None] >= jnp.arange(RESPONSE_LENGTH)[None, :]

    def group_queries(group_id):
        query_part = lax.dynamic_index_in_dim(every_query_row, group_id, 1, keepdims=False).astype(jnp.float32)
        key_part = lax.dynamic_index_in_dim(prompt_row_count, group_id, 2, keepdims=False)
        value_part = lax.dynamic_index_in_dim(prompt_value_rows, group_id, 2, keepdims=False)

        def absorb(running, kv_pair):
            top_now, total_now, sum_now = running
            key_block, value_block = kv_pair
            scores = jnp.einsum("trd,pd->trp", query_part, key_block.astype(jnp.float32)) * score_scale
            block_maximum = scores.max(-1)
            weights = jnp.exp(scores - block_maximum[..., None])
            block_total = weights.sum(-1)
            rounded = lax.optimization_barrier(weights.astype(jnp.bfloat16)).astype(jnp.float32)
            block_output = jnp.einsum("trp,pd->trd", rounded, value_block.astype(jnp.float32)) / block_total[..., None]
            block_output = lax.optimization_barrier(block_output.astype(jnp.bfloat16)).astype(jnp.float32)
            new_top = jnp.maximum(top_now, block_maximum)
            old_scale = jnp.exp(top_now - new_top)
            new_scale = block_total * jnp.exp(block_maximum - new_top)
            return (new_top, total_now * old_scale + new_scale,
                    sum_now * old_scale[..., None] + new_scale[..., None] * block_output), None

        start_state = (jnp.full((token_rows, heads_per_group), -1e30, jnp.float32),
                       jnp.zeros((token_rows, heads_per_group), jnp.float32),
                       jnp.zeros((token_rows, heads_per_group, HEAD_SIZE), jnp.float32))
        (prefix_top, prefix_total, prefix_sum), _ = lax.scan(absorb, start_state, (key_part, value_part))

        query_resp = query_part.reshape(RESPONSE_COUNT, RESPONSE_LENGTH, heads_per_group, HEAD_SIZE)
        suffix_key = lax.dynamic_index_in_dim(response_rows, group_id, 2, keepdims=False).astype(jnp.float32)
        suffix_value = lax.dynamic_index_in_dim(response_value_rows, group_id, 2, keepdims=False).astype(jnp.float32)
        scores = jnp.einsum("btrd,bjd->btrj", query_resp, suffix_key) * score_scale
        scores = jnp.where(causal[None, :, None, :], scores, -jnp.inf)
        suffix_top = scores.max(-1)
        weights = jnp.exp(scores - suffix_top[..., None])
        suffix_total = weights.sum(-1)
        rounded = lax.optimization_barrier(weights.astype(jnp.bfloat16)).astype(jnp.float32)
        suffix_out = jnp.einsum("btrj,bjd->btrd", rounded, suffix_value) / suffix_total[..., None]
        suffix_top = suffix_top.reshape(token_rows, heads_per_group)
        suffix_total = suffix_total.reshape(token_rows, heads_per_group)
        suffix_out = suffix_out.reshape(token_rows, heads_per_group, HEAD_SIZE)
        overall = jnp.maximum(prefix_top, suffix_top)
        prefix_scale = jnp.exp(prefix_top - overall)
        suffix_scale = suffix_total * jnp.exp(suffix_top - overall)
        numerator = prefix_sum * prefix_scale[..., None] + suffix_scale[..., None] * suffix_out
        denominator = prefix_total * prefix_scale + suffix_scale
        return numerator / denominator[..., None]

    head_outputs = lax.map(group_queries, jnp.arange(KEY_VALUE_HEADS))
    attended = jnp.moveaxis(head_outputs, 0, 1).reshape(token_rows, QUERY_HEADS * HEAD_SIZE)
    live_rows = (jnp.arange(RESPONSE_LENGTH)[None, :] < lengths[:, None]).reshape(token_rows)
    attended = jnp.where(live_rows[:, None], attended, 0.0).astype(jnp.bfloat16)
    return jnp.dot(attended, out_weight, preferred_element_type=jnp.float32).astype(jnp.bfloat16)
```

```python
import functools
import math

import jax
import jax.numpy as jnp
from jax import lax
from jax.experimental import pallas as pl
from jax.experimental.pallas import tpu as pltpu
from jax.sharding import Mesh, PartitionSpec as P

HEAD_SIZE = 128
F32 = jnp.float32
BF16 = jnp.bfloat16
SCORE_SCALE = HEAD_SIZE**-0.5 * math.log2(math.e)
LOWEST = -1e30
VMEM_LIMIT = 40 * 2**20
SUB_AXES = ("xh", "y", "z", "xl", "c")
PREFIX = ("z", "xl", "c")
SWAP = [(0, 1), (1, 0)]


def score_dot(q, k):
    return lax.dot_general(q, k, (((1,), (1,)), ((), ())), preferred_element_type=F32)


def absorb(state, scores, values):
    top, total, acc = state
    new_top = jnp.maximum(top, scores.max(-1, keepdims=True) * SCORE_SCALE)
    decay = jnp.exp2(top - new_top)
    weights = jnp.exp2(scores * SCORE_SCALE - new_top).astype(BF16)
    extended = jnp.concatenate([values, jnp.ones(values.shape, BF16)], axis=1)
    added = jnp.dot(weights, extended, preferred_element_type=F32)
    return new_top, total * decay + added[:, 128:129], acc * decay + added[:, :128]


def empty_state(rows):
    return (
        jnp.full((rows, 1), LOWEST, F32),
        jnp.zeros((rows, 1), F32),
        jnp.zeros((rows, HEAD_SIZE), F32),
    )


def store_state(state, acc_out, stat_out):
    top, total, acc = state
    acc_out[...] = acc
    lane = lax.broadcasted_iota(jnp.int32, acc.shape, 1)
    stat_out[...] = jnp.where(lane < 64, top, total)


def absorb_blocks(state, q, blocks, chunk):
    for block in blocks:
        for at in range(0, block.shape[1], chunk):
            keys = block[0, at : at + chunk, :]
            values = block[1, at : at + chunk, :]
            state = absorb(state, score_dot(q, keys), values)
    return state


def first_own_kernel(chunk, q_ref, rk_ref, rv_ref, block, acc_out, stat_out):
    resp_len = rk_ref.shape[1]
    row = lax.broadcasted_iota(jnp.int32, (resp_len, resp_len), 0)
    col = lax.broadcasted_iota(jnp.int32, (resp_len, resp_len), 1)
    tops, totals, accs = [], [], []
    for r in range(rk_ref.shape[0]):
        q = q_ref[r * resp_len : (r + 1) * resp_len, :]
        scores = jnp.where(row >= col, score_dot(q, rk_ref[r]), LOWEST)
        top, total, acc = absorb(empty_state(resp_len), scores, rv_ref[r])
        tops.append(top)
        totals.append(total)
        accs.append(acc)
    state = tuple(jnp.concatenate(part, axis=0) for part in (tops, totals, accs))
    state = absorb_blocks(state, q_ref[...], [block], chunk)
    store_state(state, acc_out, stat_out)


def first_other_kernel(chunk, q_ref, block, acc_in, stat_in, acc_out, stat_out):
    del acc_in, stat_in
    state = absorb_blocks(empty_state(q_ref.shape[0]), q_ref[...], [block], chunk)
    store_state(state, acc_out, stat_out)


def middle_kernel(chunk, count, q_ref, *refs):
    blocks, (acc_in, stat_in, acc_out, stat_out) = refs[:count], refs[count:]
    state = (stat_in[:, 0:1], stat_in[:, 64:65], acc_in[...])
    state = absorb_blocks(state, q_ref[...], blocks, chunk)
    store_state(state, acc_out, stat_out)


def last_kernel(chunk, count, q_ref, *refs):
    blocks, (acc_in, stat_in, out_ref, lse_ref) = refs[:count], refs[count:]
    state = (stat_in[:, 0:1], stat_in[:, 64:65], acc_in[...])
    top, total, acc = absorb_blocks(state, q_ref[...], blocks, chunk)
    out_ref[...] = (acc / total).astype(BF16)
    lse = top + jnp.log2(total)
    lse_ref[...] = jnp.broadcast_to(lse, acc.shape).T[0:8]


def attention_cost(rows, positions):
    return pl.CostEstimate(
        flops=8 * rows * positions * HEAD_SIZE,
        bytes_accessed=rows * 2048,
        transcendentals=rows * positions,
    )


def params():
    return pltpu.CompilerParams(vmem_limit_bytes=VMEM_LIMIT)


def whole(array):
    return pl.BlockSpec(array.shape, lambda i: (0,) * array.ndim)


def rows_spec(tile, offset=0):
    return pl.BlockSpec((tile, HEAD_SIZE), lambda i: (i + offset, 0))


def first_own(q, resp_k, resp_v, block, all_rows, tile, chunk):
    rows = q.shape[0]
    state = jax.ShapeDtypeStruct((all_rows, HEAD_SIZE), F32)
    return pl.pallas_call(
        functools.partial(first_own_kernel, chunk),
        grid=(rows // tile,),
        in_specs=[rows_spec(tile), whole(resp_k), whole(resp_v), whole(block)],
        out_specs=[rows_spec(tile)] * 2,
        out_shape=[state] * 2,
        cost_estimate=attention_cost(rows, block.shape[1]),
        compiler_params=params(),
        name="attend_own",
    )(q, resp_k, resp_v, block)


def first_other(q, block, state, start, tile, chunk):
    rows = q.shape[0]
    at = start // tile
    return pl.pallas_call(
        functools.partial(first_other_kernel, chunk),
        grid=(rows // tile,),
        in_specs=[rows_spec(tile), whole(block)] + [pl.BlockSpec(memory_space=pl.ANY)] * 2,
        out_specs=[rows_spec(tile, at)] * 2,
        out_shape=[jax.ShapeDtypeStruct(s.shape, s.dtype) for s in state],
        input_output_aliases={2: 0, 3: 1},
        cost_estimate=attention_cost(rows, block.shape[1]),
        compiler_params=params(),
        name="attend_first",
    )(q, block, *state)


def more(q, blocks, state, last, tile, chunk):
    rows = q.shape[0]
    count = len(blocks)
    if last:
        kernel = last_kernel
        out_specs = [rows_spec(tile), pl.BlockSpec((8, tile), lambda i: (0, i))]
        out_shape = [
            jax.ShapeDtypeStruct((rows, HEAD_SIZE), BF16),
            jax.ShapeDtypeStruct((8, rows), F32),
        ]
        aliases = {}
    else:
        kernel = middle_kernel
        out_specs = [rows_spec(tile)] * 2
        out_shape = [jax.ShapeDtypeStruct(s.shape, s.dtype) for s in state]
        aliases = {1 + count: 0, 2 + count: 1}
    return pl.pallas_call(
        functools.partial(kernel, chunk, count),
        grid=(rows // tile,),
        in_specs=[rows_spec(tile)] + [whole(b) for b in blocks] + [rows_spec(tile)] * 2,
        out_specs=out_specs,
        out_shape=out_shape,
        input_output_aliases=aliases,
        cost_estimate=attention_cost(rows, sum(b.shape[1] for b in blocks)),
        compiler_params=params(),
        name="attend_last" if last else "attend_more",
    )(q, *blocks, *state)


def pack_kernel(z_ref, k_ref, v_ref, *outs):
    groups = len(outs)
    for d in range(groups):
        group = lax.rem(z_ref[0] + d, groups)
        columns = pl.ds(pl.multiple_of(group * HEAD_SIZE, HEAD_SIZE), HEAD_SIZE)
        outs[d][0] = k_ref[:, columns]
        outs[d][1] = v_ref[:, columns]


def pack(z, keys, values):
    groups = keys.shape[1] // HEAD_SIZE
    out = jax.ShapeDtypeStruct((2, keys.shape[0], HEAD_SIZE), BF16)
    return pl.pallas_call(
        pack_kernel,
        in_specs=[
            pl.BlockSpec(memory_space=pltpu.SMEM),
            pl.BlockSpec(memory_space=pltpu.VMEM),
            pl.BlockSpec(memory_space=pltpu.VMEM),
        ],
        out_specs=[pl.BlockSpec(memory_space=pltpu.VMEM)] * groups,
        out_shape=[out] * groups,
        compiler_params=params(),
        name="pack_heads",
    )(z.reshape(1), keys, values)


def column(lse):
    return jnp.broadcast_to(lse[0:1], (HEAD_SIZE, lse.shape[1])).T


def merge(out_a, lse_a, out_b, lse_b):
    top = jnp.maximum(lse_a, lse_b)
    weight_a, weight_b = jnp.exp2(lse_a - top), jnp.exp2(lse_b - top)
    total = weight_a + weight_b
    merged = (weight_a * out_a.astype(F32) + weight_b * out_b.astype(F32)) / total
    return merged, top + jnp.log2(total)


def merge_kernel(a_ref, a_lse, b_ref, b_lse, out_ref, lse_ref):
    out, lse = merge(a_ref[...], column(a_lse), b_ref[...], column(b_lse))
    out_ref[...] = out.astype(BF16)
    lse_ref[...] = lse.T[0:8]


def final_merge_kernel(a_ref, a_lse, b_ref, b_lse, live_ref, out_ref):
    out, _ = merge(a_ref[...], column(a_lse), b_ref[...], column(b_lse))
    out_ref[...] = jnp.where(column(live_ref) > 0, out, 0.0).astype(BF16)


def merge_pair(own, other, rows, tile):
    out_spec = rows_spec(tile)
    lse_spec = pl.BlockSpec((8, tile), lambda i: (0, i))
    return pl.pallas_call(
        merge_kernel,
        grid=(rows // tile,),
        in_specs=[out_spec, lse_spec] * 2,
        out_specs=[out_spec, lse_spec],
        out_shape=[
            jax.ShapeDtypeStruct((rows, HEAD_SIZE), BF16),
            jax.ShapeDtypeStruct((8, rows), F32),
        ],
        compiler_params=params(),
        name="merge_pair",
    )(*own, *other)


def merge_final(own, other, live):
    rows = own[0].shape[0]
    tokens = live.shape[1]
    blocks = rows // tokens
    out_spec = pl.BlockSpec((tokens, HEAD_SIZE), lambda i: (i, 0))
    lse_spec = pl.BlockSpec((8, tokens), lambda i: (0, i))
    half = blocks // 2
    out_turned = pl.BlockSpec((tokens, HEAD_SIZE), lambda i: ((i + half) % blocks, 0))
    lse_turned = pl.BlockSpec((8, tokens), lambda i: (0, (i + half) % blocks))
    return pl.pallas_call(
        final_merge_kernel,
        grid=(blocks,),
        in_specs=[out_spec, lse_spec, out_turned, lse_turned, whole(live)],
        out_specs=pl.BlockSpec((tokens, HEAD_SIZE), lambda i: (0, i)),
        out_shape=jax.ShapeDtypeStruct((tokens, blocks * HEAD_SIZE), BF16),
        compiler_params=params(),
        name="merge_final",
    )(*own, *other, live)


def on_device(queries, keys, values, resp_keys, resp_values, lengths, out_weight):
    z, xl, c = (lax.axis_index(a) for a in PREFIX)
    resp_count, resp_len, features = queries.shape
    tokens = resp_count * resp_len
    tile, chunk = 512, 256
    z_size = lax.axis_size("z")

    own_heads = features // HEAD_SIZE
    own_rows = own_heads * tokens
    q_own = queries.reshape(tokens, own_heads, HEAD_SIZE)
    q_own = jnp.moveaxis(q_own, 1, 0).reshape(own_rows, HEAD_SIZE)
    q_x = lax.ppermute(q_own, "xl", SWAP)
    q_c = lax.ppermute(q_own, "c", SWAP)
    q_xc = lax.ppermute(q_x, "c", SWAP)

    packed = pack(z, keys, values)
    blocks = [packed[0]]
    for d in range(1, z_size):
        blocks.append(lax.ppermute(packed[d], "z", [(i, (i + d) % z_size) for i in range(z_size)]))

    depth, width = out_weight.shape
    quarters = out_weight.T.reshape(2, 2, width // 4, depth)
    of_c = lax.dynamic_index_in_dim(quarters, c, 1, keepdims=False)
    from_c = lax.ppermute(
        lax.dynamic_index_in_dim(quarters, 1 - c, 1, keepdims=False), "c", SWAP
    )
    both = jnp.stack([of_c, from_c], axis=1)
    mine = lax.dynamic_index_in_dim(both, xl, 0, keepdims=False)
    theirs = lax.ppermute(lax.dynamic_index_in_dim(both, 1 - xl, 0, keepdims=False), "xl", SWAP)
    weight_part = jnp.stack([mine[0], theirs[0], mine[1], theirs[1]], axis=1)
    weight_part = weight_part.reshape(width // 4, 4 * depth)
    weight = lax.all_gather(weight_part, ("xh", "y"), axis=0, tiled=True)

    head = z * HEAD_SIZE
    rk = lax.dynamic_slice_in_dim(resp_keys, head, HEAD_SIZE, 2)
    rv = lax.dynamic_slice_in_dim(resp_values, head, HEAD_SIZE, 2)

    state = first_own(q_own, rk, rv, blocks[0], 4 * own_rows, tile, chunk)
    q_rest = jnp.concatenate([q_x, q_c, q_xc], axis=0)
    state = first_other(q_rest, blocks[0], state, own_rows, tile, chunk)
    q_all = jnp.concatenate([q_own, q_rest], axis=0)
    state = more(q_all, [blocks[1], blocks[7]], state, False, tile, chunk)
    state = more(q_all, [blocks[2], blocks[6]], state, False, tile, chunk)
    out, lse = more(q_all, [blocks[3], blocks[5], blocks[4]], state, True, tile, chunk)

    half = 2 * own_rows
    sent = (lax.ppermute(out[half:], "c", SWAP), lax.ppermute(lse[:, half:], "c", SWAP))
    out, lse = merge_pair((out, lse), sent, half, tile)
    sent = (lax.ppermute(out, "xl", SWAP), lax.ppermute(lse, "xl", SWAP))
    live = (jnp.arange(resp_len)[None, :] < lengths[:, None]).astype(F32).reshape(1, tokens)
    live = jnp.broadcast_to(live, (8, tokens))
    attended = merge_final((out, lse), sent, live)
    attended_c = lax.ppermute(attended, "c", SWAP)

    depth_half = 2 * depth
    contract = (((1,), (1,)), ((), ()))
    partial = lax.dot_general(
        attended, weight[:, :depth_half], contract, preferred_element_type=F32
    ) + lax.dot_general(attended_c, weight[:, depth_half:], contract, preferred_element_type=F32)
    partial = partial.astype(BF16)

    received = lax.all_to_all(partial, PREFIX, split_axis=0, concat_axis=0, tiled=True)
    out_rows = tokens // (z_size * 4)
    received = received.reshape(z_size, 4, out_rows, -1, width // 4)
    total = received.astype(F32).sum(0).astype(BF16)
    return total.transpose(1, 2, 0, 3).reshape(out_rows, -1)


def solution(mesh):
    shape = (2, mesh.shape["batch"] // 2, mesh.shape["prefix"] // 4, 2, 2)
    fine = Mesh(mesh.devices.reshape(shape), SUB_AXES)
    batch = ("xh", "y")
    placed = (
        P(batch, None, PREFIX),
        P(PREFIX, None),
        P(PREFIX, None),
        P(batch, None, None),
        P(batch, None, None),
        P(batch),
        P(PREFIX, batch),
    )
    return jax.shard_map(
        on_device,
        mesh=fine,
        in_specs=placed,
        out_specs=P(batch + PREFIX, None),
        check_vma=False,
    )
```

```python
import functools
import math

import jax
import jax.numpy as jnp
from jax import lax
from jax.experimental import pallas as pl
from jax.experimental.pallas import tpu as pltpu
from jax.sharding import Mesh, PartitionSpec as P

HEAD_SIZE = 128
F32 = jnp.float32
BF16 = jnp.bfloat16
SCORE_SCALE = HEAD_SIZE**-0.5 * math.log2(math.e)
LOWEST = -1e30
VMEM_LIMIT = 40 * 2**20
SUB_AXES = ("xh", "y", "z", "xl", "c")
PREFIX = ("z", "xl", "c")
SWAP = [(0, 1), (1, 0)]
PARTS = 2
SLAB = 8
SLOTS = 4


def score_dot(q, k):
    return lax.dot_general(q, k, (((1,), (1,)), ((), ())), preferred_element_type=F32)


def absorb(state, scores, values):
    top, total, acc = state
    new_top = jnp.maximum(top, scores.max(-1, keepdims=True) * SCORE_SCALE)
    decay = jnp.exp2(top - new_top)
    weights = jnp.exp2(scores * SCORE_SCALE - new_top).astype(BF16)
    extended = jnp.concatenate([values, jnp.ones(values.shape, BF16)], axis=1)
    added = jnp.dot(weights, extended, preferred_element_type=F32)
    return new_top, total * decay + added[:, 128:129], acc * decay + added[:, :128]


def empty_state(rows):
    return (
        jnp.full((rows, 1), LOWEST, F32),
        jnp.zeros((rows, 1), F32),
        jnp.zeros((rows, HEAD_SIZE), F32),
    )


def store_state(state, acc_out, stat_out):
    top, total, acc = state
    acc_out[...] = acc
    lane = lax.broadcasted_iota(jnp.int32, acc.shape, 1)
    stat_out[...] = jnp.where(lane < 64, top, total)


def load_state(acc_in, stat_in):
    stat = stat_in[...]
    lane = lax.broadcasted_iota(jnp.int32, stat.shape, 1)
    top = jnp.where(lane < 64, stat, LOWEST).max(-1, keepdims=True)
    total = jnp.where(lane < 64, 0.0, stat).max(-1, keepdims=True)
    return top, total, acc_in[...]


def absorb_blocks(state, q, blocks, chunk):
    for block in blocks:
        for at in range(0, block.shape[1], chunk):
            keys = block[0, at : at + chunk, :]
            values = block[1, at : at + chunk, :]
            state = absorb(state, score_dot(q, keys), values)
    return state


def first_own_kernel(chunk, q_ref, rk_ref, rv_ref, block, acc_out, stat_out):
    count, resp_len, _ = rk_ref.shape
    part = resp_len // PARTS
    row = lax.broadcasted_iota(jnp.int32, (part, resp_len), 0)
    col = lax.broadcasted_iota(jnp.int32, (part, resp_len), 1)
    token = (row // SLAB) * (PARTS * SLAB) + pl.program_id(0) * SLAB + row % SLAB
    tops, totals, accs = [], [], []
    for at in range(0, q_ref.shape[0], part):
        r = at // part % count
        scores = score_dot(q_ref[at : at + part, :], rk_ref[r])
        scores = jnp.where(token >= col, scores, LOWEST)
        top, total, acc = absorb(empty_state(part), scores, rv_ref[r])
        tops.append(top)
        totals.append(total)
        accs.append(acc)
    state = tuple(jnp.concatenate(part, axis=0) for part in (tops, totals, accs))
    state = absorb_blocks(state, q_ref[...], [block], chunk)
    store_state(state, acc_out, stat_out)


def first_other_kernel(chunk, q_ref, block, acc_in, stat_in, acc_out, stat_out):
    del acc_in, stat_in
    state = absorb_blocks(empty_state(q_ref.shape[0]), q_ref[...], [block], chunk)
    store_state(state, acc_out, stat_out)


def middle_kernel(chunk, count, q_ref, *refs):
    blocks, (acc_in, stat_in, acc_out, stat_out) = refs[:count], refs[count:]
    state = load_state(acc_in, stat_in)
    state = absorb_blocks(state, q_ref[...], blocks, chunk)
    store_state(state, acc_out, stat_out)


def last_kernel(chunk, count, q_ref, *refs):
    blocks, (acc_in, stat_in, out_ref, lse_ref) = refs[:count], refs[count:]
    state = load_state(acc_in, stat_in)
    top, total, acc = absorb_blocks(state, q_ref[...], blocks, chunk)
    out_ref[...] = (acc / total).astype(out_ref.dtype)
    lse = top + jnp.log2(total)
    lse_ref[...] = jnp.broadcast_to(lse, acc.shape).T[0:8]


def attention_cost():
    return pl.CostEstimate(flops=1, bytes_accessed=1, transcendentals=0)


def params():
    return pltpu.CompilerParams(vmem_limit_bytes=VMEM_LIMIT)


def whole(array):
    return pl.BlockSpec(array.shape, lambda i: (0,) * array.ndim)


def rows_spec(tile, index=lambda i: i):
    return pl.BlockSpec((tile, HEAD_SIZE), lambda i: (index(i), 0))


def first_own(q, resp_k, resp_v, block):
    tile = q.shape[0] // PARTS
    state = jax.ShapeDtypeStruct((SLOTS * q.shape[0], HEAD_SIZE), F32)
    return pl.pallas_call(
        functools.partial(first_own_kernel, 512),
        grid=(PARTS,),
        in_specs=[rows_spec(tile), whole(resp_k), whole(resp_v), whole(block)],
        out_specs=[rows_spec(tile, lambda i: i * SLOTS)] * 2,
        out_shape=[state] * 2,
        cost_estimate=attention_cost(),
        compiler_params=params(),
        name="attend_own",
    )(q, resp_k, resp_v, block)


def first_other(q, block, state, chunk):
    tile = q.shape[0] // (PARTS * SLOTS)
    others = SLOTS - 1

    def index(i):
        return i // others * SLOTS + 1 + i % others

    return pl.pallas_call(
        functools.partial(first_other_kernel, chunk),
        grid=(PARTS * others,),
        in_specs=[rows_spec(tile, index), whole(block)] + [pl.BlockSpec(memory_space=pl.ANY)] * 2,
        out_specs=[rows_spec(tile, index)] * 2,
        out_shape=[jax.ShapeDtypeStruct(s.shape, s.dtype) for s in state],
        input_output_aliases={2: 0, 3: 1},
        cost_estimate=attention_cost(),
        compiler_params=params(),
        name="attend_first",
    )(q, block, *state)


def attend_more(q, blocks, state, tile, chunk):
    rows = q.shape[0]
    count = len(blocks)
    return pl.pallas_call(
        functools.partial(middle_kernel, chunk, count),
        grid=(rows // tile,),
        in_specs=[rows_spec(tile)] + [whole(b) for b in blocks] + [rows_spec(tile)] * 2,
        out_specs=[rows_spec(tile)] * 2,
        out_shape=[jax.ShapeDtypeStruct(s.shape, s.dtype) for s in state],
        input_output_aliases={1 + count: 0, 2 + count: 1},
        cost_estimate=attention_cost(),
        compiler_params=params(),
        name="attend_more",
    )(q, *blocks, *state)


def attend_last(q, blocks, state, start, rows, tile, chunk, dtype):
    count = len(blocks)
    at = start // tile
    moved = rows_spec(tile, lambda i: i + at)
    return pl.pallas_call(
        functools.partial(last_kernel, chunk, count),
        grid=(rows // tile,),
        in_specs=[moved] + [whole(b) for b in blocks] + [moved] * 2,
        out_specs=[rows_spec(tile), pl.BlockSpec((8, tile), lambda i: (0, i))],
        out_shape=[
            jax.ShapeDtypeStruct((rows, HEAD_SIZE), dtype),
            jax.ShapeDtypeStruct((8, rows), F32),
        ],
        cost_estimate=attention_cost(),
        compiler_params=params(),
        name="attend_last",
    )(q, *blocks, *state)


def pack_kernel(z_ref, half_ref, k_ref, v_ref, *outs):
    groups = len(outs)
    for d in range(groups):
        group = lax.rem(z_ref[0] + d, groups)
        columns = pl.ds(pl.multiple_of(group * HEAD_SIZE, HEAD_SIZE), HEAD_SIZE)
        count = outs[d].shape[1]
        start = pl.multiple_of(half_ref[0] * count, count) if d else 0
        outs[d][0] = k_ref[pl.ds(start, count), columns]
        outs[d][1] = v_ref[pl.ds(start, count), columns]


def pack(z, half, keys, values):
    groups = keys.shape[1] // HEAD_SIZE
    count = keys.shape[0]
    out = jax.ShapeDtypeStruct((2, count, HEAD_SIZE), BF16)
    out_half = jax.ShapeDtypeStruct((2, count // 2, HEAD_SIZE), BF16)
    return pl.pallas_call(
        pack_kernel,
        in_specs=[pl.BlockSpec(memory_space=pltpu.SMEM)] * 2
        + [pl.BlockSpec(memory_space=pltpu.VMEM)] * 2,
        out_specs=[pl.BlockSpec(memory_space=pltpu.VMEM)] * groups,
        out_shape=[out] + [out_half] * (groups - 1),
        cost_estimate=attention_cost(),
        compiler_params=params(),
        name="pack_heads",
    )(z.reshape(1), half.reshape(1), keys, values)


def column(lse):
    return jnp.broadcast_to(lse[0:1], (HEAD_SIZE, lse.shape[1])).T


def merge(out_a, lse_a, out_b, lse_b):
    top = jnp.maximum(lse_a, lse_b)
    weight_a, weight_b = jnp.exp2(lse_a - top), jnp.exp2(lse_b - top)
    total = weight_a + weight_b
    merged = (weight_a * out_a.astype(F32) + weight_b * out_b.astype(F32)) / total
    return merged, top + jnp.log2(total)


def merge_kernel(a_ref, a_lse, b_ref, b_lse, out_ref, sent_ref, lse_ref):
    out, lse = merge(a_ref[...], column(a_lse), b_ref[...], column(b_lse))
    out_ref[...] = out
    sent_ref[...] = out.astype(BF16)
    lse_ref[...] = lse.T[0:8]


def final_merge_kernel(a_ref, a_lse, b_ref, b_lse, live_ref, out_ref):
    out, _ = merge(a_ref[...], column(a_lse), b_ref[...], column(b_lse))
    out_ref[...] = jnp.where(column(live_ref) > 0, out, 0.0).astype(BF16)


def merge_pair(own, other, tile):
    rows = other[0].shape[0]
    out_spec = rows_spec(tile)
    lse_spec = pl.BlockSpec((8, tile), lambda i: (0, i))
    return pl.pallas_call(
        merge_kernel,
        grid=(rows // tile,),
        in_specs=[out_spec, lse_spec] * 2,
        out_specs=[out_spec, out_spec, lse_spec],
        out_shape=[
            jax.ShapeDtypeStruct((rows, HEAD_SIZE), F32),
            jax.ShapeDtypeStruct((rows, HEAD_SIZE), BF16),
            jax.ShapeDtypeStruct((8, rows), F32),
        ],
        cost_estimate=attention_cost(),
        compiler_params=params(),
        name="merge_pair",
    )(*own, *other)


def merge_final(own, other, live):
    rows = own[0].shape[0]
    tokens = live.shape[1]
    blocks = rows // tokens
    out_spec = pl.BlockSpec((tokens, HEAD_SIZE), lambda i: (i, 0))
    lse_spec = pl.BlockSpec((8, tokens), lambda i: (0, i))
    half = blocks // 2
    out_turned = pl.BlockSpec((tokens, HEAD_SIZE), lambda i: ((i + half) % blocks, 0))
    lse_turned = pl.BlockSpec((8, tokens), lambda i: (0, (i + half) % blocks))
    return pl.pallas_call(
        final_merge_kernel,
        grid=(blocks,),
        in_specs=[out_spec, lse_spec, out_turned, lse_turned, whole(live)],
        out_specs=pl.BlockSpec((tokens, HEAD_SIZE), lambda i: (0, i)),
        out_shape=jax.ShapeDtypeStruct((tokens, blocks * HEAD_SIZE), BF16),
        cost_estimate=attention_cost(),
        compiler_params=params(),
        name="merge_final",
    )(*own, *other, live)


def on_device(queries, keys, values, resp_keys, resp_values, lengths, out_weight):
    y, z, xl, c = (lax.axis_index(a) for a in ("y",) + PREFIX)
    resp_count, resp_len, features = queries.shape
    tokens = resp_count * resp_len
    tile, chunk = 1024, 256
    z_size, y_size = lax.axis_size("z"), lax.axis_size("y")
    own_heads = features // HEAD_SIZE
    part_tokens = tokens // PARTS
    slot_rows = own_heads * part_tokens

    packed = pack(z, y % 2, keys, values)
    q_own = queries.reshape(-1, PARTS, SLAB, own_heads, HEAD_SIZE)
    q_own = q_own.transpose(1, 3, 0, 2, 4).reshape(PARTS * slot_rows, HEAD_SIZE)
    q_x = lax.ppermute(q_own, "xl", SWAP)
    q_c = lax.ppermute(q_own, "c", SWAP)
    q_xc = lax.ppermute(q_x, "c", SWAP)

    blocks = {0: [packed[0]]}
    for d in (1, 7, 2, 6, 3, 5, 4):
        half = lax.ppermute(packed[d], "z", [(i, (i + d) % z_size) for i in range(z_size)])
        blocks[d] = [half, lax.ppermute(half, "y", [(i, i ^ 1) for i in range(y_size)])]

    depth, width = out_weight.shape
    quarters = out_weight.T.reshape(2, 2, width // 4, depth)
    of_c = lax.dynamic_index_in_dim(quarters, c, 1, keepdims=False)
    from_c = lax.ppermute(
        lax.dynamic_index_in_dim(quarters, 1 - c, 1, keepdims=False), "c", SWAP
    )
    both = jnp.stack([of_c, from_c], axis=1)
    mine = lax.dynamic_index_in_dim(both, xl, 0, keepdims=False)
    theirs = lax.ppermute(lax.dynamic_index_in_dim(both, 1 - xl, 0, keepdims=False), "xl", SWAP)
    weight_part = jnp.stack([mine[0], theirs[0], mine[1], theirs[1]], axis=1)
    weight_part = weight_part.reshape(width // 4, 4 * depth)
    weight = lax.all_gather(weight_part, ("xh", "y"), axis=0, tiled=True)

    head = z * HEAD_SIZE
    rk = lax.dynamic_slice_in_dim(resp_keys, head, HEAD_SIZE, 2)
    rv = lax.dynamic_slice_in_dim(resp_values, head, HEAD_SIZE, 2)

    state = first_own(q_own, rk, rv, blocks[0][0])
    slots = [q.reshape(PARTS, 1, slot_rows, HEAD_SIZE) for q in (q_own, q_x, q_c, q_xc)]
    q_all = jnp.concatenate(slots, axis=1).reshape(-1, HEAD_SIZE)
    state = first_other(q_all, blocks[0][0], state, chunk)
    state = attend_more(q_all, blocks[1] + blocks[7], state, tile, chunk)
    state = attend_more(q_all, blocks[2] + blocks[6], state, tile, chunk)
    rest = blocks[3] + blocks[5] + blocks[4]

    resp_pos = jnp.arange(tokens).reshape(-1, PARTS, SLAB)
    live = (resp_pos % resp_len < jnp.take(lengths, resp_pos // resp_len)).astype(F32)
    depth_half = 2 * depth
    contract = (((1,), (1,)), ((), ()))
    results = []
    half = 2 * slot_rows
    for part in range(PARTS):
        at = part * SLOTS * slot_rows
        far = attend_last(q_all, rest, state, at + half, half, 512, chunk, BF16)
        far = tuple(lax.ppermute(a, "c", SWAP) for a in far)
        near = attend_last(q_all, rest, state, at, half, 512, chunk, F32)
        out, sent, lse = merge_pair(near, far, 512)
        other = (lax.ppermute(sent, "xl", SWAP), lax.ppermute(lse, "xl", SWAP))
        part_live = jnp.broadcast_to(live[:, part].reshape(1, part_tokens), (8, part_tokens))
        attended = merge_final((out, lse), other, part_live)
        attended_c = lax.ppermute(attended, "c", SWAP)
        partial = lax.dot_general(
            attended, weight[:, :depth_half], contract, preferred_element_type=F32
        ) + lax.dot_general(
            attended_c, weight[:, depth_half:], contract, preferred_element_type=F32
        )
        partial = partial.astype(BF16)
        received = lax.all_to_all(partial, PREFIX, split_axis=0, concat_axis=0, tiled=True)
        received = received.reshape(z_size, SLOTS, SLAB, -1, width // 4)
        total = received.astype(F32).sum(0).astype(BF16)
        results.append(total.transpose(1, 2, 0, 3).reshape(SLAB, -1))
    return jnp.concatenate(results, axis=0)


def solution(mesh):
    shape = (2, mesh.shape["batch"] // 2, mesh.shape["prefix"] // 4, 2, 2)
    fine = Mesh(mesh.devices.reshape(shape), SUB_AXES)
    batch = ("xh", "y")
    placed = (
        P(batch, None, PREFIX),
        P(PREFIX, None),
        P(PREFIX, None),
        P(batch, None, None),
        P(batch, None, None),
        P(batch),
        P(PREFIX, batch),
    )
    return jax.shard_map(
        on_device,
        mesh=fine,
        in_specs=placed,
        out_specs=P(batch + PREFIX, None),
        check_vma=False,
    )
```

```python
import functools
import math

import jax
import jax.numpy as jnp
from jax import lax
from jax.experimental import pallas as pl
from jax.experimental.pallas import tpu as pltpu
from jax.sharding import Mesh, PartitionSpec as P

HEAD_SIZE = 128
LANES = 128
F32 = jnp.float32
BF16 = jnp.bfloat16
SCORE_SCALE = HEAD_SIZE**-0.5 * math.log2(math.e)
LOWEST = -1e30
VMEM_LIMIT = 24 * 2**20
SUB_AXES = ("xh", "y", "z", "xl", "c")
PREFIX = ("z", "xl", "c")
SWAP = [(0, 1), (1, 0)]
PARTS = 2
SLAB = 8
SLOTS = 4
STAT_ROWS = 16
CHUNK = 256
FLOPS_PER_MICRO = 1.15e9


def score_dot(q, k):
    return lax.dot_general(q, k, (((1,), (1,)), ((), ())), preferred_element_type=F32)


def absorb(state, scores, values):
    top, total, acc = state
    new_top = jnp.maximum(top, scores.max(-1, keepdims=True) * SCORE_SCALE)
    decay = jnp.exp2(top - new_top)
    weights = jnp.exp2(scores * SCORE_SCALE - new_top).astype(BF16)
    extended = jnp.concatenate([values, jnp.ones(values.shape, BF16)], axis=1)
    added = jnp.dot(weights, extended, preferred_element_type=F32)
    return new_top, total * decay + added[:, 128:129], acc * decay + added[:, :128]


def empty_state(rows):
    return (
        jnp.full((rows, 1), LOWEST, F32),
        jnp.zeros((rows, 1), F32),
        jnp.zeros((rows, HEAD_SIZE), F32),
    )


def store_state(state, acc_out, stat_out):
    top, total, acc = state
    acc_out[...] = acc
    lane = lax.broadcasted_iota(jnp.int32, acc.shape, 1)
    stat_out[...] = jnp.where(lane < 64, top, total)


def load_state(acc_in, stat_in):
    stat = stat_in[...]
    lane = lax.broadcasted_iota(jnp.int32, stat.shape, 1)
    top = jnp.where(lane < 64, stat, LOWEST).max(-1, keepdims=True)
    total = jnp.where(lane < 64, 0.0, stat).max(-1, keepdims=True)
    return top, total, acc_in[...]


def absorb_block(state, q, keys, values, chunk=CHUNK):
    count = keys.shape[0]
    for at in range(0, count, chunk):
        to = min(at + chunk, count)
        state = absorb(state, score_dot(q, keys[at:to, :]), values[at:to, :])
    return state


def first_own_kernel(q_ref, rk_ref, rv_ref, block, acc_out, stat_out):
    count, resp_len, _ = rk_ref.shape
    part = resp_len // PARTS
    row = lax.broadcasted_iota(jnp.int32, (part, resp_len), 0)
    col = lax.broadcasted_iota(jnp.int32, (part, resp_len), 1)
    token = (row // SLAB) * (PARTS * SLAB) + pl.program_id(0) * SLAB + row % SLAB
    tops, totals, accs = [], [], []
    for at in range(0, q_ref.shape[0], part):
        r = at // part % count
        scores = score_dot(q_ref[at : at + part, :], rk_ref[r])
        scores = jnp.where(token >= col, scores, LOWEST)
        top, total, acc = absorb(empty_state(part), scores, rv_ref[r])
        tops.append(top)
        totals.append(total)
        accs.append(acc)
    state = tuple(jnp.concatenate(part, axis=0) for part in (tops, totals, accs))
    state = absorb_block(state, q_ref[...], block.at[0], block.at[1], 512)
    store_state(state, acc_out, stat_out)


def first_all_kernel(q_ref, block, near_block, acc_in, stat_in, acc_out, stat_out):
    rows = q_ref.shape[0]
    own_rows = acc_in.shape[0]
    own = pl.program_id(0) % (SLOTS * own_rows // rows) == 0

    def absorb_first(start):
        state = empty_state(rows - start)
        state = absorb_block(state, q_ref[start:, :], block.at[0], block.at[1])
        store_state(state, acc_out.at[start:, :], stat_out.at[start:, :])

    @pl.when(own)
    def _():
        acc_out[:own_rows, :] = acc_in[...]
        stat_out[:own_rows, :] = stat_in[...]
        absorb_first(own_rows)

    @pl.when(jnp.logical_not(own))
    def _():
        absorb_first(0)

    state = load_state(acc_out, stat_out)
    state = absorb_block(state, q_ref[...], near_block.at[0], near_block.at[1])
    store_state(state, acc_out, stat_out)


def narrow(columns):
    rows = columns.shape[0]
    lines = []
    for at in range(0, rows, LANES):
        wide = jnp.broadcast_to(columns[at : at + LANES], (LANES, LANES))
        lines.append(wide.T[0:1])
    lines.append(jnp.zeros((STAT_ROWS - rows // LANES, LANES), F32))
    return jnp.concatenate(lines, axis=0)


def widen(lines, rows):
    columns = []
    for i in range(rows // LANES):
        columns.append(jnp.broadcast_to(lines[i : i + 1], (LANES, LANES)).T)
    return jnp.concatenate(columns, axis=0)


def store_sent(sent_ref, out, lines):
    rows = out.shape[0]
    sent_ref[0:rows, :] = out.astype(BF16)
    for i in range(3):
        term = lines.astype(BF16)
        sent_ref[rows + i * STAT_ROWS : rows + (i + 1) * STAT_ROWS, :] = term
        lines = lines - term.astype(F32)


def load_sent(sent_ref):
    rows = sent_ref.shape[0] - 3 * STAT_ROWS
    lines = jnp.zeros((STAT_ROWS, LANES), F32)
    for i in range(3):
        term = sent_ref[rows + i * STAT_ROWS : rows + (i + 1) * STAT_ROWS, :]
        lines = lines + term.astype(F32)
    return sent_ref[0:rows, :].astype(F32), widen(lines, rows)


def merge(out_a, lse_a, out_b, lse_b):
    top = jnp.maximum(lse_a, lse_b)
    weight_a, weight_b = jnp.exp2(lse_a - top), jnp.exp2(lse_b - top)
    total = weight_a + weight_b
    return (weight_a * out_a + weight_b * out_b) / total, top + jnp.log2(total)


def finish(q_ref, blocks, acc_in, stat_in):
    state = load_state(acc_in, stat_in)
    for block in blocks:
        state = absorb_block(state, q_ref[...], block.at[0], block.at[1])
    top, total, acc = state
    return acc / total, top + jnp.log2(total)


def far_kernel(q_ref, acc_in, stat_in, *refs):
    blocks, sent_ref = refs[:-1], refs[-1]
    out, lse = finish(q_ref, blocks, acc_in, stat_in)
    store_sent(sent_ref, out, narrow(lse))


def near_kernel(q_ref, acc_in, stat_in, *refs):
    blocks, (got_ref, out_ref, lines_ref, sent_ref) = refs[:-4], refs[-4:]
    out, lse = finish(q_ref, blocks, acc_in, stat_in)
    out, lse = merge(out, jnp.broadcast_to(lse, out.shape), *load_sent(got_ref))
    lines = narrow(lse[:, 0:1])
    out_ref[...] = out
    lines_ref[...] = lines
    store_sent(sent_ref, out, lines)


def last_merge_kernel(part, lengths_ref, out_ref, lines_ref, got_ref, attended_ref):
    tokens, width = attended_ref.shape
    rows = out_ref.shape[0]
    half = rows // 2
    got, got_lse = load_sent(got_ref)
    got = jnp.concatenate([got[half:], got[:half]], axis=0)
    got_lse = jnp.concatenate([got_lse[half:], got_lse[:half]], axis=0)
    out, _ = merge(out_ref[...], widen(lines_ref[...], rows), got, got_lse)
    row = lax.broadcasted_iota(jnp.int32, (tokens, LANES), 0)
    count = lengths_ref.shape[0]
    per = tokens // count
    token = (row % per) // SLAB * (PARTS * SLAB) + part * SLAB + row % SLAB
    valid = jnp.zeros((tokens, LANES), jnp.int32)
    for r in range(count):
        valid = jnp.where(row // per == r, lengths_ref[r], valid)
    live = token < valid
    for i in range(width // HEAD_SIZE):
        head = jnp.where(live, out[i * tokens : (i + 1) * tokens], 0.0)
        attended_ref[:, i * HEAD_SIZE : (i + 1) * HEAD_SIZE] = head.astype(BF16)


def project_kernel(w_ref, *refs):
    pairs, out_ref = refs[:-1], refs[-1]
    devices, _, rows, width = out_ref.shape
    depth = w_ref.shape[1] // 4
    for part in range(PARTS):
        product = 0.0
        for i in range(4):
            ref, at = pairs[2 * part + i % 2], i // 2 * depth
            weight = w_ref[:, i * depth : (i + 1) * depth]
            product = product + score_dot(ref[:, at : at + depth], weight)
        out_ref[:, part] = product.reshape(devices, rows, width).astype(BF16)


def total_kernel(blocks, xh_ref, *refs):
    parts, out_ref = refs[:-1], refs[-1]
    half = out_ref.shape[1] // 2
    lines = []
    for ref in parts:
        count, rows, columns = ref.shape
        sums = ref[...].astype(F32).reshape(count // SLOTS, SLOTS, rows, columns).sum(0)
        piece = columns // blocks
        turned = []
        for rel in range(2):
            starts = range(rel * piece, columns, 2 * piece)
            pieces = [sums[q][:, at : at + piece] for at in starts for q in range(SLOTS)]
            turned.append(jnp.concatenate(pieces, axis=1))
        lines.append(turned)
    here = jnp.concatenate([line[0] for line in lines], axis=0).astype(BF16)
    there = jnp.concatenate([line[1] for line in lines], axis=0).astype(BF16)
    at_here = pl.multiple_of(xh_ref[0] * half, half)
    at_there = pl.multiple_of((1 - xh_ref[0]) * half, half)
    out_ref[:, pl.ds(at_here, half)] = here
    out_ref[:, pl.ds(at_there, half)] = there


def call(kernel, name, micros, order=(), in_specs=(), **options):
    def run(*operands):
        held = jnp.zeros((1,), jnp.int32)
        if order:
            held = after(held, *order)
        return pl.pallas_call(
            lambda held_ref, *refs: kernel(*refs),
            name=name,
            in_specs=[SMEM, *in_specs],
            cost_estimate=pl.CostEstimate(
                flops=int(micros * FLOPS_PER_MICRO), bytes_accessed=1, transcendentals=0
            ),
            compiler_params=pltpu.CompilerParams(vmem_limit_bytes=VMEM_LIMIT),
            **options,
        )(held, *operands)

    return run


def whole(array):
    return pl.BlockSpec(array.shape, lambda i: (0,) * array.ndim)


def rows_spec(tile, index=lambda i: i):
    return pl.BlockSpec((tile, HEAD_SIZE), lambda i: (index(i), 0))


def shapes_of(arrays):
    return [jax.ShapeDtypeStruct(a.shape, a.dtype) for a in arrays]


VMEM = pl.BlockSpec(memory_space=pltpu.VMEM)
SMEM = pl.BlockSpec(memory_space=pltpu.SMEM)


def first_own(q, resp_k, resp_v, block, order):
    tile = q.shape[0] // PARTS
    state = jax.ShapeDtypeStruct(q.shape, F32)
    return call(
        first_own_kernel,
        "attend_own",
        5,
        order,
        grid=(PARTS,),
        in_specs=[rows_spec(tile), whole(resp_k), whole(resp_v), whole(block)],
        out_specs=[rows_spec(tile)] * 2,
        out_shape=[state] * 2,
    )(q, resp_k, resp_v, block)


def first_all(q, block, near_block, own_state, tile, order):
    own_rows = q.shape[0] // (PARTS * SLOTS)
    state = jax.ShapeDtypeStruct(q.shape, F32)
    tiles = q.shape[0] // tile
    held = rows_spec(own_rows, lambda i: i * PARTS // tiles)
    return call(
        first_all_kernel,
        "attend_first",
        11,
        order,
        grid=(tiles,),
        in_specs=[rows_spec(tile), whole(block), whole(near_block), held, held],
        out_specs=[rows_spec(tile)] * 2,
        out_shape=[state] * 2,
    )(q, block, near_block, *own_state)


def attend_far(q, blocks, state, part, rows, order):
    moved = rows_spec(rows, lambda i: 2 * part + 1)
    sent = jax.ShapeDtypeStruct((rows + 3 * STAT_ROWS, HEAD_SIZE), BF16)
    return call(
        far_kernel,
        "attend_far",
        5,
        order,
        grid=(1,),
        in_specs=[moved] * 3 + [whole(b) for b in blocks],
        out_specs=whole(sent),
        out_shape=sent,
    )(q, *state, *blocks)


def attend_near(q, blocks, state, got, part, rows, order):
    moved = rows_spec(rows, lambda i: 2 * part)
    out_shape = [
        jax.ShapeDtypeStruct((rows, HEAD_SIZE), F32),
        jax.ShapeDtypeStruct((STAT_ROWS, LANES), F32),
        jax.ShapeDtypeStruct(got.shape, BF16),
    ]
    return call(
        near_kernel,
        "attend_near",
        5,
        order,
        grid=(1,),
        in_specs=[moved] * 3 + [whole(b) for b in blocks] + [whole(got)],
        out_specs=[whole(s) for s in out_shape],
        out_shape=out_shape,
    )(q, *state, *blocks, got)


def last_merge(part, lengths, out, lines, got, tokens, order):
    attended = jax.ShapeDtypeStruct((tokens, out.shape[0] // tokens * HEAD_SIZE), BF16)
    return call(
        functools.partial(last_merge_kernel, part),
        "merge_last",
        1,
        order,
        grid=(1,),
        in_specs=[SMEM] + [whole(a) for a in (out, lines, got)],
        out_specs=whole(attended),
        out_shape=attended,
    )(lengths, out, lines, got)


def project(pairs, weight, tile=640):
    devices = pairs[0].shape[0] // SLAB
    columns, depth = weight.shape
    return call(
        project_kernel,
        "project",
        3,
        grid=(columns // tile,),
        in_specs=[pl.BlockSpec((tile, depth), lambda i: (i, 0))] + [whole(a) for a in pairs],
        out_specs=pl.BlockSpec((devices, PARTS, SLAB, tile), lambda i: (0, 0, 0, i)),
        out_shape=jax.ShapeDtypeStruct((devices, PARTS, SLAB, columns), BF16),
    )(weight, *pairs)


def add_up(xh, parts, width, blocks):
    rows = sum(part.shape[1] for part in parts)
    out = jax.ShapeDtypeStruct((rows, width), BF16)
    return call(
        functools.partial(total_kernel, blocks),
        "add_up",
        2,
        grid=(1,),
        in_specs=[SMEM] + [whole(p) for p in parts],
        out_specs=whole(out),
        out_shape=out,
    )(xh.reshape(1), *parts)


def pack_kernel(z_ref, y_ref, k_ref, v_ref, own_ref, *outs):
    groups = len(outs) + 1
    here = pl.ds(pl.multiple_of(z_ref[0] * HEAD_SIZE, HEAD_SIZE), HEAD_SIZE)
    own_ref[0] = k_ref[:, here]
    own_ref[1] = v_ref[:, here]
    for d, out in enumerate(outs, 1):
        count = out.shape[1]
        rows = pl.ds(pl.multiple_of(y_ref[0] * count, count), count)
        group = lax.rem(z_ref[0] + d, groups)
        columns = pl.ds(pl.multiple_of(group * HEAD_SIZE, HEAD_SIZE), HEAD_SIZE)
        out[0] = k_ref[rows, columns]
        out[1] = v_ref[rows, columns]


def pack(z, y, y_size, keys, values):
    groups = keys.shape[1] // HEAD_SIZE
    count = keys.shape[0]
    own = jax.ShapeDtypeStruct((2, count, HEAD_SIZE), BF16)
    sent = jax.ShapeDtypeStruct((2, count // y_size, HEAD_SIZE), BF16)
    out_shape = [own] + [sent] * (groups - 1)
    return call(
        pack_kernel,
        "pack_heads",
        2,
        grid=(1,),
        in_specs=[SMEM] * 2 + [whole(keys), whole(values)],
        out_specs=[whole(s) for s in out_shape],
        out_shape=out_shape,
    )(z.reshape(1), y.reshape(1), keys, values)


def unpack_kernel(*refs):
    blocks, out_ref = refs[:-1], refs[-1]
    for i, block in enumerate(blocks):
        count = block.shape[1]
        out_ref[0, i * count : (i + 1) * count] = block[0]
        out_ref[1, i * count : (i + 1) * count] = block[1]


def unpack(blocks, order):
    two, count, width = blocks[0].shape
    out = jax.ShapeDtypeStruct((two, len(blocks) * count, width), BF16)
    return call(
        unpack_kernel,
        "unpack_heads",
        1,
        order,
        grid=(1,),
        in_specs=[whole(b) for b in blocks],
        out_specs=whole(out),
        out_shape=out,
    )(*blocks)


def after(array, *others):
    return lax.optimization_barrier((array, *others))[0]


def weight_of_core(out_weight, c):
    depth, width = out_weight.shape
    quarters = out_weight.T.reshape(2, 2, width // 4, depth)
    of_c = lax.dynamic_index_in_dim(quarters, c, 1, keepdims=False)
    sent = lax.dynamic_index_in_dim(quarters, 1 - c, 1, keepdims=False)
    return jnp.concatenate([of_c, lax.ppermute(sent, "c", SWAP)], axis=2)


def on_device(queries, keys, values, resp_keys, resp_values, lengths, out_weight):
    xh, y, z, xl, c = (lax.axis_index(a) for a in SUB_AXES)
    resp_count, resp_len, features = queries.shape
    tokens = resp_count * resp_len
    y_size, z_size = lax.axis_size("y"), lax.axis_size("z")
    own_heads = features // HEAD_SIZE
    part_tokens = tokens // PARTS
    slot_rows = own_heads * part_tokens
    width = out_weight.shape[1]

    both = weight_of_core(out_weight, c)
    w_own = lax.dynamic_index_in_dim(both, xl, 0, keepdims=False)
    w_sent = lax.dynamic_index_in_dim(both, 1 - xl, 0, keepdims=False)
    w_x = lax.ppermute(w_sent, "xl", SWAP)
    w_h = lax.ppermute(w_own, "xh", SWAP)
    w_xh = lax.ppermute(w_sent, ("xh", "xl"), [(i, 3 - i) for i in range(4)])
    own_block, *sent = pack(z, y, y_size, keys, values)
    *sent, _ = lax.optimization_barrier((*sent, both))
    got = []
    for d in (4, 5, 3, 6, 2, 7, 1):
        got.append(lax.ppermute(sent[d - 1], "z", [(i, (i + d) % z_size) for i in range(z_size)]))

    q_own = after(queries, own_block).reshape(-1, PARTS, SLAB, own_heads, HEAD_SIZE)
    q_own = q_own.transpose(1, 3, 0, 2, 4).reshape(PARTS * slot_rows, HEAD_SIZE)
    q_x = lax.ppermute(q_own, "xl", SWAP)
    q_c = lax.ppermute(q_own, "c", SWAP)

    near_y = unpack(got, (w_x, w_h, w_xh))
    up = [(i, (i + 1) % y_size) for i in range(y_size)]
    down = [(i, (i - 1) % y_size) for i in range(y_size)]
    from_below = lax.ppermute(near_y, "y", up)
    from_above = lax.ppermute(near_y, "y", down)

    head = z * HEAD_SIZE
    rk = lax.dynamic_slice_in_dim(resp_keys, head, HEAD_SIZE, 2)
    rv = lax.dynamic_slice_in_dim(resp_values, head, HEAD_SIZE, 2)
    state = first_own(q_own, rk, rv, own_block, (near_y,))
    w_own = after(w_own, state[0])
    here = jnp.concatenate([w_own, w_x], axis=1)
    there = jnp.concatenate([w_h, w_xh], axis=1)
    weight = lax.all_gather(jnp.concatenate([here, there], axis=0), "y", axis=0, tiled=True)

    q_xc = lax.ppermute(after(q_x, state[0]), "c", SWAP)
    slots = [q.reshape(PARTS, 1, slot_rows, HEAD_SIZE) for q in (q_own, q_x, q_c, q_xc)]
    q_all = jnp.concatenate(slots, axis=1).reshape(-1, HEAD_SIZE)
    state = first_all(q_all, own_block, near_y, state, 1024, (from_below,))
    across = lax.ppermute(from_below, "y", up)
    half = 2 * slot_rows
    blocks = [from_below, from_above, across]
    far = []
    for part in range(PARTS):
        order = (far[-1],) if far else ()
        far.append(attend_far(q_all, blocks, state, part, half, order))
    far_c = [lax.ppermute(f, "c", SWAP) for f in far]
    near, near_x, merged = [], [], []
    for part in range(PARTS):
        order = (near[-1][0],) if near else (far[-1],)
        out, lines, sent = attend_near(q_all, blocks, state, far_c[part], part, half, order)
        near.append((out, lines))
        near_x.append(lax.ppermute(sent, "xl", SWAP))
    for part in range(PARTS - 1):
        merged.append(
            last_merge(part, lengths, *near[part], near_x[part], part_tokens, (near[-1][0],))
        )
    merged.append(
        last_merge(PARTS - 1, lengths, *near[-1], near_x[-1], part_tokens, (merged[-1],))
    )
    pairs = []
    for attended in merged:
        pairs += [attended, lax.ppermute(attended, "c", SWAP)]
    partial = project(pairs, weight)
    partial = partial.reshape(partial.shape[0], PARTS * SLAB, partial.shape[-1])
    received = lax.all_to_all(partial, PREFIX, split_axis=0, concat_axis=0, tiled=True)
    blocks = 2 * y_size
    return add_up(xh, [received], width * blocks, blocks)


def solution(mesh):
    shape = (2, mesh.shape["batch"] // 2, mesh.shape["prefix"] // 4, 2, 2)
    fine = Mesh(mesh.devices.reshape(shape), SUB_AXES)
    batch = ("xh", "y")
    placed = (
        P(batch, None, PREFIX),
        P(PREFIX, None),
        P(PREFIX, None),
        P(batch, None, None),
        P(batch, None, None),
        P(batch),
        P(PREFIX, batch),
    )
    return jax.shard_map(
        on_device,
        mesh=fine,
        in_specs=placed,
        out_specs=P(batch + PREFIX, None),
        check_vma=False,
    )
```

```python
import functools
import math

import jax
import jax.numpy as jnp
from jax import lax
from jax.experimental import pallas as pl
from jax.experimental.pallas import tpu as pltpu
from jax.sharding import Mesh, PartitionSpec as P

HEAD_SIZE = 128
LANES = 128
F32 = jnp.float32
BF16 = jnp.bfloat16
SCORE_SCALE = HEAD_SIZE**-0.5 * math.log2(math.e)
LOWEST = -1e30
VMEM_LIMIT = 24 * 2**20
SUB_AXES = ("xh", "y", "z", "xl", "c")
PREFIX = ("z", "xl", "c")
SWAP = [(0, 1), (1, 0)]
PARTS = 2
SLAB = 8
SLOTS = 4
STAT_ROWS = 16
CHUNK = 256
FLOPS_PER_MICRO = 1.15e9


def score_dot(q, k):
    return lax.dot_general(q, k, (((1,), (1,)), ((), ())), preferred_element_type=F32)


def absorb(state, scores, values):
    top, total, acc = state
    new_top = jnp.maximum(top, scores.max(-1, keepdims=True) * SCORE_SCALE)
    decay = jnp.exp2(top - new_top)
    weights = jnp.exp2(scores * SCORE_SCALE - new_top).astype(BF16)
    extended = jnp.concatenate([values, jnp.ones(values.shape, BF16)], axis=1)
    added = jnp.dot(weights, extended, preferred_element_type=F32)
    return new_top, total * decay + added[:, 128:129], acc * decay + added[:, :128]


def empty_state(rows):
    return (
        jnp.full((rows, 1), LOWEST, F32),
        jnp.zeros((rows, 1), F32),
        jnp.zeros((rows, HEAD_SIZE), F32),
    )


def store_state(state, acc_out, stat_out):
    top, total, acc = state
    acc_out[...] = acc
    lane = lax.broadcasted_iota(jnp.int32, acc.shape, 1)
    stat_out[...] = jnp.where(lane < 64, top, total)


def load_state(acc_in, stat_in):
    stat = stat_in[...]
    lane = lax.broadcasted_iota(jnp.int32, stat.shape, 1)
    top = jnp.where(lane < 64, stat, LOWEST).max(-1, keepdims=True)
    total = jnp.where(lane < 64, 0.0, stat).max(-1, keepdims=True)
    return top, total, acc_in[...]


def absorb_block(state, q, keys, values, chunk=CHUNK):
    count = keys.shape[0]
    for at in range(0, count, chunk):
        to = min(at + chunk, count)
        state = absorb(state, score_dot(q, keys[at:to, :]), values[at:to, :])
    return state


def first_own_kernel(q_ref, rk_ref, rv_ref, block, acc_out, stat_out):
    count, resp_len, _ = rk_ref.shape
    part = resp_len // PARTS
    row = lax.broadcasted_iota(jnp.int32, (part, resp_len), 0)
    col = lax.broadcasted_iota(jnp.int32, (part, resp_len), 1)
    token = (row // SLAB) * (PARTS * SLAB) + pl.program_id(0) * SLAB + row % SLAB
    tops, totals, accs = [], [], []
    for at in range(0, q_ref.shape[0], part):
        r = at // part % count
        scores = score_dot(q_ref[at : at + part, :], rk_ref[r])
        scores = jnp.where(token >= col, scores, LOWEST)
        top, total, acc = absorb(empty_state(part), scores, rv_ref[r])
        tops.append(top)
        totals.append(total)
        accs.append(acc)
    state = tuple(jnp.concatenate(part, axis=0) for part in (tops, totals, accs))
    state = absorb_block(state, q_ref[...], block.at[0], block.at[1], 512)
    store_state(state, acc_out, stat_out)


def first_all_kernel(q_ref, block, near_block, acc_in, stat_in, acc_out, stat_out):
    rows = q_ref.shape[0]
    own_rows = acc_in.shape[0]
    own = pl.program_id(0) % (SLOTS * own_rows // rows) == 0

    def absorb_first(start):
        state = empty_state(rows - start)
        state = absorb_block(state, q_ref[start:, :], block.at[0], block.at[1])
        store_state(state, acc_out.at[start:, :], stat_out.at[start:, :])

    @pl.when(own)
    def _():
        acc_out[:own_rows, :] = acc_in[...]
        stat_out[:own_rows, :] = stat_in[...]
        absorb_first(own_rows)

    @pl.when(jnp.logical_not(own))
    def _():
        absorb_first(0)

    state = load_state(acc_out, stat_out)
    state = absorb_block(state, q_ref[...], near_block.at[0], near_block.at[1])
    store_state(state, acc_out, stat_out)


def middle_kernel(count, q_ref, *refs):
    blocks, (acc_in, stat_in, acc_out, stat_out) = refs[:count], refs[count:]
    state = load_state(acc_in, stat_in)
    for block in blocks:
        state = absorb_block(state, q_ref[...], block.at[0], block.at[1])
    store_state(state, acc_out, stat_out)


def narrow(columns):
    rows = columns.shape[0]
    lines = []
    for at in range(0, rows, LANES):
        wide = jnp.broadcast_to(columns[at : at + LANES], (LANES, LANES))
        lines.append(wide.T[0:1])
    lines.append(jnp.zeros((STAT_ROWS - rows // LANES, LANES), F32))
    return jnp.concatenate(lines, axis=0)


def widen(lines, rows):
    columns = []
    for i in range(rows // LANES):
        columns.append(jnp.broadcast_to(lines[i : i + 1], (LANES, LANES)).T)
    return jnp.concatenate(columns, axis=0)


def store_sent(sent_ref, out, lines):
    rows = out.shape[0]
    sent_ref[0:rows, :] = out.astype(BF16)
    for i in range(3):
        term = lines.astype(BF16)
        sent_ref[rows + i * STAT_ROWS : rows + (i + 1) * STAT_ROWS, :] = term
        lines = lines - term.astype(F32)


def load_sent(sent_ref):
    rows = sent_ref.shape[0] - 3 * STAT_ROWS
    lines = jnp.zeros((STAT_ROWS, LANES), F32)
    for i in range(3):
        term = sent_ref[rows + i * STAT_ROWS : rows + (i + 1) * STAT_ROWS, :]
        lines = lines + term.astype(F32)
    return sent_ref[0:rows, :].astype(F32), widen(lines, rows)


def merge(out_a, lse_a, out_b, lse_b):
    top = jnp.maximum(lse_a, lse_b)
    weight_a, weight_b = jnp.exp2(lse_a - top), jnp.exp2(lse_b - top)
    total = weight_a + weight_b
    return (weight_a * out_a + weight_b * out_b) / total, top + jnp.log2(total)


def finish(q_ref, blocks, acc_in, stat_in):
    state = load_state(acc_in, stat_in)
    keys, values = blocks
    top, total, acc = absorb_block(state, q_ref[...], keys, values)
    return acc / total, top + jnp.log2(total)


def far_kernel(q_ref, acc_in, stat_in, *refs):
    blocks, sent_ref = refs[:-1], refs[-1]
    out, lse = finish(q_ref, blocks, acc_in, stat_in)
    store_sent(sent_ref, out, narrow(lse))


def near_kernel(q_ref, acc_in, stat_in, *refs):
    blocks, (got_ref, out_ref, lines_ref, sent_ref) = refs[:-4], refs[-4:]
    out, lse = finish(q_ref, blocks, acc_in, stat_in)
    out, lse = merge(out, jnp.broadcast_to(lse, out.shape), *load_sent(got_ref))
    lines = narrow(lse[:, 0:1])
    out_ref[...] = out
    lines_ref[...] = lines
    store_sent(sent_ref, out, lines)


def last_merge_kernel(part, lengths_ref, out_ref, lines_ref, got_ref, attended_ref):
    tokens, width = attended_ref.shape
    rows = out_ref.shape[0]
    half = rows // 2
    got, got_lse = load_sent(got_ref)
    got = jnp.concatenate([got[half:], got[:half]], axis=0)
    got_lse = jnp.concatenate([got_lse[half:], got_lse[:half]], axis=0)
    out, _ = merge(out_ref[...], widen(lines_ref[...], rows), got, got_lse)
    row = lax.broadcasted_iota(jnp.int32, (tokens, LANES), 0)
    count = lengths_ref.shape[0]
    per = tokens // count
    token = (row % per) // SLAB * (PARTS * SLAB) + part * SLAB + row % SLAB
    valid = jnp.zeros((tokens, LANES), jnp.int32)
    for r in range(count):
        valid = jnp.where(row // per == r, lengths_ref[r], valid)
    live = token < valid
    for i in range(width // HEAD_SIZE):
        head = jnp.where(live, out[i * tokens : (i + 1) * tokens], 0.0)
        attended_ref[:, i * HEAD_SIZE : (i + 1) * HEAD_SIZE] = head.astype(BF16)


def project_kernel(w_ref, *refs):
    pairs, out_ref = refs[:-1], refs[-1]
    devices, _, rows, width = out_ref.shape
    depth = w_ref.shape[1] // 4
    for part in range(PARTS):
        product = 0.0
        for i in range(4):
            ref, at = pairs[2 * part + i % 2], i // 2 * depth
            weight = w_ref[:, i * depth : (i + 1) * depth]
            product = product + score_dot(ref[:, at : at + depth], weight)
        out_ref[:, part] = product.reshape(devices, rows, width).astype(BF16)


def total_kernel(blocks, xh_ref, *refs):
    parts, out_ref = refs[:-1], refs[-1]
    half = out_ref.shape[1] // 2
    lines = []
    for ref in parts:
        count, rows, columns = ref.shape
        sums = ref[...].astype(F32).reshape(count // SLOTS, SLOTS, rows, columns).sum(0)
        piece = columns // blocks
        turned = []
        for rel in range(2):
            starts = range(rel * piece, columns, 2 * piece)
            pieces = [sums[q][:, at : at + piece] for at in starts for q in range(SLOTS)]
            turned.append(jnp.concatenate(pieces, axis=1))
        lines.append(turned)
    here = jnp.concatenate([line[0] for line in lines], axis=0).astype(BF16)
    there = jnp.concatenate([line[1] for line in lines], axis=0).astype(BF16)
    at_here = pl.multiple_of(xh_ref[0] * half, half)
    at_there = pl.multiple_of((1 - xh_ref[0]) * half, half)
    out_ref[:, pl.ds(at_here, half)] = here
    out_ref[:, pl.ds(at_there, half)] = there


def call(kernel, name, micros, order=(), in_specs=(), **options):
    def run(*operands):
        held = jnp.zeros((1,), jnp.int32)
        if order:
            held = after(held, *order)
        return pl.pallas_call(
            lambda held_ref, *refs: kernel(*refs),
            name=name,
            in_specs=[SMEM, *in_specs],
            cost_estimate=pl.CostEstimate(
                flops=int(micros * FLOPS_PER_MICRO), bytes_accessed=1, transcendentals=0
            ),
            compiler_params=pltpu.CompilerParams(vmem_limit_bytes=VMEM_LIMIT),
            **options,
        )(held, *operands)

    return run


def whole(array):
    return pl.BlockSpec(array.shape, lambda i: (0,) * array.ndim)


def rows_spec(tile, index=lambda i: i):
    return pl.BlockSpec((tile, HEAD_SIZE), lambda i: (index(i), 0))


def shapes_of(arrays):
    return [jax.ShapeDtypeStruct(a.shape, a.dtype) for a in arrays]


VMEM = pl.BlockSpec(memory_space=pltpu.VMEM)
SMEM = pl.BlockSpec(memory_space=pltpu.SMEM)


def first_own(q, resp_k, resp_v, block, order):
    tile = q.shape[0] // PARTS
    state = jax.ShapeDtypeStruct(q.shape, F32)
    return call(
        first_own_kernel,
        "attend_own",
        5,
        order,
        grid=(PARTS,),
        in_specs=[rows_spec(tile), whole(resp_k), whole(resp_v), whole(block)],
        out_specs=[rows_spec(tile)] * 2,
        out_shape=[state] * 2,
    )(q, resp_k, resp_v, block)


def first_all(q, block, near_block, own_state, tile, order):
    own_rows = q.shape[0] // (PARTS * SLOTS)
    state = jax.ShapeDtypeStruct(q.shape, F32)
    tiles = q.shape[0] // tile
    held = rows_spec(own_rows, lambda i: i * PARTS // tiles)
    return call(
        first_all_kernel,
        "attend_first",
        11,
        order,
        grid=(tiles,),
        in_specs=[rows_spec(tile), whole(block), whole(near_block), held, held],
        out_specs=[rows_spec(tile)] * 2,
        out_shape=[state] * 2,
    )(q, block, near_block, *own_state)


def attend_more(q, blocks, state, tile, order, start=0, rows=None):
    rows = rows or q.shape[0]
    count = len(blocks)
    at = start // tile
    moved = rows_spec(tile, lambda i: i + at)
    return call(
        functools.partial(middle_kernel, count),
        "attend_more",
        7 * count * rows // q.shape[0],
        order,
        grid=(rows // tile,),
        in_specs=[moved] + [whole(b) for b in blocks] + [moved] * 2,
        out_specs=[rows_spec(tile)] * 2,
        out_shape=[jax.ShapeDtypeStruct((rows, HEAD_SIZE), F32)] * 2,
    )(q, *blocks, *state)


def attend_far(q, blocks, state, part, rows, order):
    moved = rows_spec(rows, lambda i: 2 * part + 1)
    sent = jax.ShapeDtypeStruct((rows + 3 * STAT_ROWS, HEAD_SIZE), BF16)
    return call(
        far_kernel,
        "attend_far",
        2,
        order,
        grid=(1,),
        in_specs=[moved] * 3 + [whole(b) for b in blocks],
        out_specs=whole(sent),
        out_shape=sent,
    )(q, *state, *blocks)


def attend_near(q, blocks, state, got, part, rows, order):
    moved = rows_spec(rows, lambda i: 2 * part)
    out_shape = [
        jax.ShapeDtypeStruct((rows, HEAD_SIZE), F32),
        jax.ShapeDtypeStruct((STAT_ROWS, LANES), F32),
        jax.ShapeDtypeStruct(got.shape, BF16),
    ]
    return call(
        near_kernel,
        "attend_near",
        2,
        order,
        grid=(1,),
        in_specs=[moved] * 3 + [whole(b) for b in blocks] + [whole(got)],
        out_specs=[whole(s) for s in out_shape],
        out_shape=out_shape,
    )(q, *state, *blocks, got)


def last_merge(part, lengths, out, lines, got, tokens, order):
    attended = jax.ShapeDtypeStruct((tokens, out.shape[0] // tokens * HEAD_SIZE), BF16)
    return call(
        functools.partial(last_merge_kernel, part),
        "merge_last",
        1,
        order,
        grid=(1,),
        in_specs=[SMEM] + [whole(a) for a in (out, lines, got)],
        out_specs=whole(attended),
        out_shape=attended,
    )(lengths, out, lines, got)


def project(pairs, weight, tile=640):
    devices = pairs[0].shape[0] // SLAB
    columns, depth = weight.shape
    return call(
        project_kernel,
        "project",
        3,
        grid=(columns // tile,),
        in_specs=[pl.BlockSpec((tile, depth), lambda i: (i, 0))] + [whole(a) for a in pairs],
        out_specs=pl.BlockSpec((devices, PARTS, SLAB, tile), lambda i: (0, 0, 0, i)),
        out_shape=jax.ShapeDtypeStruct((devices, PARTS, SLAB, columns), BF16),
    )(weight, *pairs)


def add_up(xh, parts, width, blocks):
    rows = sum(part.shape[1] for part in parts)
    out = jax.ShapeDtypeStruct((rows, width), BF16)
    return call(
        functools.partial(total_kernel, blocks),
        "add_up",
        2,
        grid=(1,),
        in_specs=[SMEM] + [whole(p) for p in parts],
        out_specs=whole(out),
        out_shape=out,
    )(xh.reshape(1), *parts)


def pack_kernel(z_ref, y_ref, k_ref, v_ref, own_ref, sent_ref):
    groups, _, count, _ = sent_ref.shape
    here = pl.ds(pl.multiple_of(z_ref[0] * HEAD_SIZE, HEAD_SIZE), HEAD_SIZE)
    own_ref[0] = k_ref[:, here]
    own_ref[1] = v_ref[:, here]
    rows = pl.ds(pl.multiple_of(y_ref[0] * count, count), count)
    for group in range(groups):
        columns = slice(group * HEAD_SIZE, (group + 1) * HEAD_SIZE)
        sent_ref[group, 0] = k_ref[rows, columns]
        sent_ref[group, 1] = v_ref[rows, columns]


def pack(z, y, y_size, keys, values):
    groups = keys.shape[1] // HEAD_SIZE
    count = keys.shape[0]
    out_shape = [
        jax.ShapeDtypeStruct((2, count, HEAD_SIZE), BF16),
        jax.ShapeDtypeStruct((groups, 2, count // y_size, HEAD_SIZE), BF16),
    ]
    return call(
        pack_kernel,
        "pack_heads",
        2,
        grid=(1,),
        in_specs=[SMEM] * 2 + [whole(keys), whole(values)],
        out_specs=[whole(s) for s in out_shape],
        out_shape=out_shape,
    )(z.reshape(1), y.reshape(1), keys, values)


def unpack_kernel(z_ref, got_ref, out_ref):
    groups, _, count, _ = got_ref.shape
    for i in range(groups - 1):
        source = lax.rem(z_ref[0] + 1 + i, groups)
        out_ref[0, i * count : (i + 1) * count] = got_ref[source, 0]
        out_ref[1, i * count : (i + 1) * count] = got_ref[source, 1]


def unpack(z, got):
    groups, two, count, width = got.shape
    out = jax.ShapeDtypeStruct((two, (groups - 1) * count, width), BF16)
    return call(
        unpack_kernel,
        "unpack_heads",
        1,
        grid=(1,),
        in_specs=[SMEM, whole(got)],
        out_specs=whole(out),
        out_shape=out,
    )(z.reshape(1), got)


def after(array, *others):
    return lax.optimization_barrier((array, *others))[0]


def weight_of_core(out_weight, c):
    depth, width = out_weight.shape
    quarters = out_weight.T.reshape(2, 2, width // 4, depth)
    of_c = lax.dynamic_index_in_dim(quarters, c, 1, keepdims=False)
    sent = lax.dynamic_index_in_dim(quarters, 1 - c, 1, keepdims=False)
    return jnp.concatenate([of_c, lax.ppermute(sent, "c", SWAP)], axis=2)


def on_device(queries, keys, values, resp_keys, resp_values, lengths, out_weight):
    xh, y, z, xl, c = (lax.axis_index(a) for a in SUB_AXES)
    resp_count, resp_len, features = queries.shape
    tokens = resp_count * resp_len
    y_size = lax.axis_size("y")
    own_heads = features // HEAD_SIZE
    part_tokens = tokens // PARTS
    slot_rows = own_heads * part_tokens
    width = out_weight.shape[1]

    both = weight_of_core(out_weight, c)
    w_own = lax.dynamic_index_in_dim(both, xl, 0, keepdims=False)
    w_sent = lax.dynamic_index_in_dim(both, 1 - xl, 0, keepdims=False)
    w_x = lax.ppermute(w_sent, "xl", SWAP)
    w_h = lax.ppermute(w_own, "xh", SWAP)
    w_xh = lax.ppermute(w_sent, ("xh", "xl"), [(i, 3 - i) for i in range(4)])
    own_block, sent = pack(z, y, y_size, keys, values)
    got = lax.all_to_all(after(sent, both), "z", split_axis=0, concat_axis=0, tiled=True)

    q_own = after(queries, own_block).reshape(-1, PARTS, SLAB, own_heads, HEAD_SIZE)
    q_own = q_own.transpose(1, 3, 0, 2, 4).reshape(PARTS * slot_rows, HEAD_SIZE)
    q_every = lax.all_gather(q_own, ("xl", "c"), axis=0, tiled=False)

    up = [(i, (i + 1) % y_size) for i in range(y_size)]
    down = [(i, (i - 1) % y_size) for i in range(y_size)]
    head = z * HEAD_SIZE
    rk = lax.dynamic_slice_in_dim(resp_keys, head, HEAD_SIZE, 2)
    rv = lax.dynamic_slice_in_dim(resp_values, head, HEAD_SIZE, 2)
    state = first_own(q_own, rk, rv, own_block, (w_x, w_h, w_xh))
    near_y = unpack(z, after(got, state[0]))
    from_below = lax.ppermute(near_y, "y", up)
    from_above = lax.ppermute(near_y, "y", down)
    here = jnp.concatenate([w_own, w_x], axis=1)
    there = jnp.concatenate([w_h, w_xh], axis=1)
    weight = lax.all_gather(jnp.concatenate([here, there], axis=0), "y", axis=0, tiled=True)

    q_every = after(q_every, state[0])
    mine = 2 * xl + c
    slots = [q_own] + [
        lax.dynamic_index_in_dim(q_every, mine ^ i, 0, keepdims=False) for i in (2, 1, 3)
    ]
    slots = [q.reshape(PARTS, 1, slot_rows, HEAD_SIZE) for q in slots]
    q_all = jnp.concatenate(slots, axis=1).reshape(-1, HEAD_SIZE)
    state = first_all(q_all, own_block, near_y, state, 1024, ())
    far_k = lax.ppermute(after(from_below, state[0])[0], "y", up)
    far_v = lax.ppermute(after(from_above, state[0])[1], "y", down)
    state = attend_more(q_all, [from_below, from_above], state, 1024, ())
    half = 2 * slot_rows
    blocks = [far_k, far_v]
    far = []
    for part in range(PARTS):
        order = (far[-1],) if far else ()
        far.append(attend_far(q_all, blocks, state, part, half, order))
    far_c = [lax.ppermute(f, "c", SWAP) for f in far]
    near, near_x, merged = [], [], []
    for part in range(PARTS):
        order = (near[-1][0],) if near else (far[-1],)
        out, lines, sent = attend_near(q_all, blocks, state, far_c[part], part, half, order)
        near.append((out, lines))
        near_x.append(lax.ppermute(sent, "xl", SWAP))
    for part in range(PARTS - 1):
        merged.append(
            last_merge(part, lengths, *near[part], near_x[part], part_tokens, (near[-1][0], weight))
        )
    merged.append(
        last_merge(PARTS - 1, lengths, *near[-1], near_x[-1], part_tokens, (merged[-1],))
    )
    pairs = []
    for attended in merged:
        pairs += [attended, lax.ppermute(attended, "c", SWAP)]
    partial = project(pairs, weight)
    partial = partial.reshape(partial.shape[0], PARTS * SLAB, partial.shape[-1])
    received = lax.all_to_all(partial, PREFIX, split_axis=0, concat_axis=0, tiled=True)
    blocks = 2 * y_size
    return add_up(xh, [received], width * blocks, blocks)


def solution(mesh):
    shape = (2, mesh.shape["batch"] // 2, mesh.shape["prefix"] // 4, 2, 2)
    fine = Mesh(mesh.devices.reshape(shape), SUB_AXES)
    batch = ("xh", "y")
    placed = (
        P(batch, None, PREFIX),
        P(PREFIX, None),
        P(PREFIX, None),
        P(batch, None, None),
        P(batch, None, None),
        P(batch),
        P(PREFIX, batch),
    )
    return jax.shard_map(
        on_device,
        mesh=fine,
        in_specs=placed,
        out_specs=P(batch + PREFIX, None),
        check_vma=False,
    )
```

```python
import functools
import math

import jax
import jax.numpy as jnp
from jax import lax
from jax.experimental import pallas as pl
from jax.experimental.pallas import tpu as pltpu
from jax.sharding import Mesh, PartitionSpec as P

HEAD_SIZE = 128
LANES = 128
F32 = jnp.float32
BF16 = jnp.bfloat16
SCORE_SCALE = HEAD_SIZE**-0.5 * math.log2(math.e)
LOWEST = -1e30
VMEM_LIMIT = 24 * 2**20
SUB_AXES = ("xh", "y", "z", "xl", "c")
PREFIX = ("z", "xl", "c")
SWAP = [(0, 1), (1, 0)]
PARTS = 2
SLAB = 8
SLOTS = 4
STAT_ROWS = 16
CHUNK = 256
FLOPS_PER_MICRO = 1.15e9


def score_dot(q, k):
    return lax.dot_general(q, k, (((1,), (1,)), ((), ())), preferred_element_type=F32)


def absorb(state, scores, values):
    top, total, acc = state
    new_top = jnp.maximum(top, scores.max(-1, keepdims=True) * SCORE_SCALE)
    decay = jnp.exp2(top - new_top)
    weights = jnp.exp2(scores * SCORE_SCALE - new_top).astype(BF16)
    extended = jnp.concatenate([values, jnp.ones(values.shape, BF16)], axis=1)
    added = jnp.dot(weights, extended, preferred_element_type=F32)
    return new_top, total * decay + added[:, 128:129], acc * decay + added[:, :128]


def empty_state(rows):
    return (
        jnp.full((rows, 1), LOWEST, F32),
        jnp.zeros((rows, 1), F32),
        jnp.zeros((rows, HEAD_SIZE), F32),
    )


def store_state(state, acc_out, stat_out):
    top, total, acc = state
    acc_out[...] = acc
    lane = lax.broadcasted_iota(jnp.int32, acc.shape, 1)
    stat_out[...] = jnp.where(lane < 64, top, total)


def load_state(acc_in, stat_in):
    stat = stat_in[...]
    lane = lax.broadcasted_iota(jnp.int32, stat.shape, 1)
    top = jnp.where(lane < 64, stat, LOWEST).max(-1, keepdims=True)
    total = jnp.where(lane < 64, 0.0, stat).max(-1, keepdims=True)
    return top, total, acc_in[...]


def rows_of(pieces):
    parts = [ref[at:to, :] for ref, at, to in pieces]
    return parts[0] if len(parts) == 1 else jnp.concatenate(parts, axis=0)


def absorb_blocks(state, q, blocks, chunk=CHUNK):
    sizes = [keys.shape[0] for keys, _ in blocks]
    ends = [sum(sizes[: i + 1]) for i in range(len(sizes))]
    at = 0
    while at < ends[-1]:
        to = min(at + chunk, ends[-1])
        spans = []
        for (keys, values), end, size in zip(blocks, ends, sizes):
            low, high = max(at, end - size), min(to, end)
            if low < high:
                spans.append((keys, values, low - end + size, high - end + size))
        keys = rows_of([(k, low, high) for k, _, low, high in spans])
        values = rows_of([(v, low, high) for _, v, low, high in spans])
        state = absorb(state, score_dot(q, keys), values)
        at = to
    return state


def absorb_block(state, q, keys, values, chunk=CHUNK):
    return absorb_blocks(state, q, [(keys, values)], chunk)


def first_own_kernel(q_ref, rk_ref, rv_ref, block, acc_out, stat_out):
    count, resp_len, _ = rk_ref.shape
    part = resp_len // PARTS
    row = lax.broadcasted_iota(jnp.int32, (part, resp_len), 0)
    col = lax.broadcasted_iota(jnp.int32, (part, resp_len), 1)
    token = (row // SLAB) * (PARTS * SLAB) + pl.program_id(0) * SLAB + row % SLAB
    tops, totals, accs = [], [], []
    for at in range(0, q_ref.shape[0], part):
        r = at // part % count
        scores = score_dot(q_ref[at : at + part, :], rk_ref[r])
        scores = jnp.where(token >= col, scores, LOWEST)
        top, total, acc = absorb(empty_state(part), scores, rv_ref[r])
        tops.append(top)
        totals.append(total)
        accs.append(acc)
    state = tuple(jnp.concatenate(part, axis=0) for part in (tops, totals, accs))
    state = absorb_block(state, q_ref[...], block.at[0], block.at[1], 512)
    store_state(state, acc_out, stat_out)


def first_all_kernel(q_ref, block, near_block, acc_in, stat_in, acc_out, stat_out):
    rows = q_ref.shape[0]
    own_rows = acc_in.shape[0]
    own = pl.program_id(0) % (SLOTS * own_rows // rows) == 0

    def absorb_first(start):
        state = empty_state(rows - start)
        state = absorb_block(state, q_ref[start:, :], block.at[0], block.at[1])
        store_state(state, acc_out.at[start:, :], stat_out.at[start:, :])

    @pl.when(own)
    def _():
        acc_out[:own_rows, :] = acc_in[...]
        stat_out[:own_rows, :] = stat_in[...]
        absorb_first(own_rows)

    @pl.when(jnp.logical_not(own))
    def _():
        absorb_first(0)

    state = load_state(acc_out, stat_out)
    state = absorb_block(state, q_ref[...], near_block.at[0], near_block.at[1])
    store_state(state, acc_out, stat_out)


def middle_kernel(count, q_ref, *refs):
    blocks, (acc_in, stat_in, acc_out, stat_out) = refs[:count], refs[count:]
    state = load_state(acc_in, stat_in)
    pairs = [(block.at[0], block.at[1]) for block in blocks]
    state = absorb_blocks(state, q_ref[...], pairs)
    store_state(state, acc_out, stat_out)


def narrow(columns):
    rows = columns.shape[0]
    lines = []
    for at in range(0, rows, LANES):
        wide = jnp.broadcast_to(columns[at : at + LANES], (LANES, LANES))
        lines.append(wide.T[0:1])
    lines.append(jnp.zeros((STAT_ROWS - rows // LANES, LANES), F32))
    return jnp.concatenate(lines, axis=0)


def widen(lines, rows):
    columns = []
    for i in range(rows // LANES):
        columns.append(jnp.broadcast_to(lines[i : i + 1], (LANES, LANES)).T)
    return jnp.concatenate(columns, axis=0)


def store_sent(sent_ref, out, lines):
    rows = out.shape[0]
    sent_ref[0:rows, :] = out.astype(BF16)
    for i in range(3):
        term = lines.astype(BF16)
        sent_ref[rows + i * STAT_ROWS : rows + (i + 1) * STAT_ROWS, :] = term
        lines = lines - term.astype(F32)


def load_sent(sent_ref):
    rows = sent_ref.shape[0] - 3 * STAT_ROWS
    lines = jnp.zeros((STAT_ROWS, LANES), F32)
    for i in range(3):
        term = sent_ref[rows + i * STAT_ROWS : rows + (i + 1) * STAT_ROWS, :]
        lines = lines + term.astype(F32)
    return sent_ref[0:rows, :].astype(F32), widen(lines, rows)


def merge(out_a, lse_a, out_b, lse_b):
    top = jnp.maximum(lse_a, lse_b)
    weight_a, weight_b = jnp.exp2(lse_a - top), jnp.exp2(lse_b - top)
    total = weight_a + weight_b
    return (weight_a * out_a + weight_b * out_b) / total, top + jnp.log2(total)


def finish(q_ref, blocks, acc_in, stat_in):
    state = load_state(acc_in, stat_in)
    keys, values = blocks
    top, total, acc = absorb_block(state, q_ref[...], keys, values)
    return acc / total, top + jnp.log2(total)


def far_kernel(q_ref, acc_in, stat_in, *refs):
    blocks, sent_ref = refs[:-1], refs[-1]
    out, lse = finish(q_ref, blocks, acc_in, stat_in)
    store_sent(sent_ref, out, narrow(lse))


def near_kernel(q_ref, acc_in, stat_in, *refs):
    blocks, (got_ref, out_ref, lines_ref, sent_ref) = refs[:-4], refs[-4:]
    out, lse = finish(q_ref, blocks, acc_in, stat_in)
    out, lse = merge(out, jnp.broadcast_to(lse, out.shape), *load_sent(got_ref))
    lines = narrow(lse[:, 0:1])
    out_ref[...] = out
    lines_ref[...] = lines
    store_sent(sent_ref, out, lines)


def last_merge_kernel(part, lengths_ref, out_ref, lines_ref, got_ref, attended_ref):
    tokens, width = attended_ref.shape
    rows = out_ref.shape[0]
    half = rows // 2
    got, got_lse = load_sent(got_ref)
    got = jnp.concatenate([got[half:], got[:half]], axis=0)
    got_lse = jnp.concatenate([got_lse[half:], got_lse[:half]], axis=0)
    out, _ = merge(out_ref[...], widen(lines_ref[...], rows), got, got_lse)
    row = lax.broadcasted_iota(jnp.int32, (tokens, LANES), 0)
    count = lengths_ref.shape[0]
    per = tokens // count
    token = (row % per) // SLAB * (PARTS * SLAB) + part * SLAB + row % SLAB
    valid = jnp.zeros((tokens, LANES), jnp.int32)
    for r in range(count):
        valid = jnp.where(row // per == r, lengths_ref[r], valid)
    live = token < valid
    for i in range(width // HEAD_SIZE):
        head = jnp.where(live, out[i * tokens : (i + 1) * tokens], 0.0)
        attended_ref[:, i * HEAD_SIZE : (i + 1) * HEAD_SIZE] = head.astype(BF16)


def project_kernel(w_ref, *refs):
    pairs, out_ref = refs[:-1], refs[-1]
    devices, _, rows, width = out_ref.shape
    depth = w_ref.shape[1] // 4
    for part in range(PARTS):
        product = 0.0
        for i in range(4):
            ref, at = pairs[2 * part + i % 2], i // 2 * depth
            weight = w_ref[:, i * depth : (i + 1) * depth]
            product = product + score_dot(ref[:, at : at + depth], weight)
        out_ref[:, part] = product.reshape(devices, rows, width).astype(BF16)


def total_kernel(blocks, xh_ref, *refs):
    parts, out_ref = refs[:-1], refs[-1]
    half = out_ref.shape[1] // 2
    lines = []
    for ref in parts:
        count, rows, columns = ref.shape
        sums = ref[...].astype(F32).reshape(count // SLOTS, SLOTS, rows, columns).sum(0)
        piece = columns // blocks
        turned = []
        for rel in range(2):
            starts = range(rel * piece, columns, 2 * piece)
            pieces = [sums[q][:, at : at + piece] for at in starts for q in range(SLOTS)]
            turned.append(jnp.concatenate(pieces, axis=1))
        lines.append(turned)
    here = jnp.concatenate([line[0] for line in lines], axis=0).astype(BF16)
    there = jnp.concatenate([line[1] for line in lines], axis=0).astype(BF16)
    at_here = pl.multiple_of(xh_ref[0] * half, half)
    at_there = pl.multiple_of((1 - xh_ref[0]) * half, half)
    out_ref[:, pl.ds(at_here, half)] = here
    out_ref[:, pl.ds(at_there, half)] = there


def call(kernel, name, micros, order=(), in_specs=(), **options):
    def run(*operands):
        held = jnp.zeros((1,), jnp.int32)
        if order:
            held = after(held, *order)
        return pl.pallas_call(
            lambda held_ref, *refs: kernel(*refs),
            name=name,
            in_specs=[SMEM, *in_specs],
            cost_estimate=pl.CostEstimate(
                flops=int(micros * FLOPS_PER_MICRO), bytes_accessed=1, transcendentals=0
            ),
            compiler_params=pltpu.CompilerParams(vmem_limit_bytes=VMEM_LIMIT),
            **options,
        )(held, *operands)

    return run


def whole(array):
    return pl.BlockSpec(array.shape, lambda i: (0,) * array.ndim)


def rows_spec(tile, index=lambda i: i):
    return pl.BlockSpec((tile, HEAD_SIZE), lambda i: (index(i), 0))


def shapes_of(arrays):
    return [jax.ShapeDtypeStruct(a.shape, a.dtype) for a in arrays]


VMEM = pl.BlockSpec(memory_space=pltpu.VMEM)
SMEM = pl.BlockSpec(memory_space=pltpu.SMEM)


def first_own(q, resp_k, resp_v, block, order):
    tile = q.shape[0] // PARTS
    state = jax.ShapeDtypeStruct(q.shape, F32)
    return call(
        first_own_kernel,
        "attend_own",
        5,
        order,
        grid=(PARTS,),
        in_specs=[rows_spec(tile), whole(resp_k), whole(resp_v), whole(block)],
        out_specs=[rows_spec(tile)] * 2,
        out_shape=[state] * 2,
    )(q, resp_k, resp_v, block)


def first_all(q, block, near_block, own_state, tile, order):
    own_rows = q.shape[0] // (PARTS * SLOTS)
    state = jax.ShapeDtypeStruct(q.shape, F32)
    tiles = q.shape[0] // tile
    held = rows_spec(own_rows, lambda i: i * PARTS // tiles)
    return call(
        first_all_kernel,
        "attend_first",
        11,
        order,
        grid=(tiles,),
        in_specs=[rows_spec(tile), whole(block), whole(near_block), held, held],
        out_specs=[rows_spec(tile)] * 2,
        out_shape=[state] * 2,
    )(q, block, near_block, *own_state)


def attend_more(q, blocks, state, tile, order, start=0, rows=None):
    rows = rows or q.shape[0]
    count = len(blocks)
    at = start // tile
    moved = rows_spec(tile, lambda i: i + at)
    return call(
        functools.partial(middle_kernel, count),
        "attend_more",
        7 * count * rows // q.shape[0],
        order,
        grid=(rows // tile,),
        in_specs=[moved] + [whole(b) for b in blocks] + [moved] * 2,
        out_specs=[rows_spec(tile)] * 2,
        out_shape=[jax.ShapeDtypeStruct((rows, HEAD_SIZE), F32)] * 2,
    )(q, *blocks, *state)


def attend_far(q, blocks, state, part, rows, order):
    moved = rows_spec(rows, lambda i: 2 * part + 1)
    sent = jax.ShapeDtypeStruct((rows + 3 * STAT_ROWS, HEAD_SIZE), BF16)
    return call(
        far_kernel,
        "attend_far",
        2,
        order,
        grid=(1,),
        in_specs=[moved] * 3 + [whole(b) for b in blocks],
        out_specs=whole(sent),
        out_shape=sent,
    )(q, *state, *blocks)


def attend_near(q, blocks, state, got, part, rows, order):
    moved = rows_spec(rows, lambda i: 2 * part)
    out_shape = [
        jax.ShapeDtypeStruct((rows, HEAD_SIZE), F32),
        jax.ShapeDtypeStruct((STAT_ROWS, LANES), F32),
        jax.ShapeDtypeStruct(got.shape, BF16),
    ]
    return call(
        near_kernel,
        "attend_near",
        2,
        order,
        grid=(1,),
        in_specs=[moved] * 3 + [whole(b) for b in blocks] + [whole(got)],
        out_specs=[whole(s) for s in out_shape],
        out_shape=out_shape,
    )(q, *state, *blocks, got)


def last_merge(part, lengths, out, lines, got, tokens, order):
    attended = jax.ShapeDtypeStruct((tokens, out.shape[0] // tokens * HEAD_SIZE), BF16)
    return call(
        functools.partial(last_merge_kernel, part),
        "merge_last",
        1,
        order,
        grid=(1,),
        in_specs=[SMEM] + [whole(a) for a in (out, lines, got)],
        out_specs=whole(attended),
        out_shape=attended,
    )(lengths, out, lines, got)


def project(pairs, weight, tile=640):
    devices = pairs[0].shape[0] // SLAB
    columns, depth = weight.shape
    return call(
        project_kernel,
        "project",
        3,
        grid=(columns // tile,),
        in_specs=[pl.BlockSpec((tile, depth), lambda i: (i, 0))] + [whole(a) for a in pairs],
        out_specs=pl.BlockSpec((devices, PARTS, SLAB, tile), lambda i: (0, 0, 0, i)),
        out_shape=jax.ShapeDtypeStruct((devices, PARTS, SLAB, columns), BF16),
    )(weight, *pairs)


def add_up(xh, parts, width, blocks):
    rows = sum(part.shape[1] for part in parts)
    out = jax.ShapeDtypeStruct((rows, width), BF16)
    return call(
        functools.partial(total_kernel, blocks),
        "add_up",
        2,
        grid=(1,),
        in_specs=[SMEM] + [whole(p) for p in parts],
        out_specs=whole(out),
        out_shape=out,
    )(xh.reshape(1), *parts)


def pack_kernel(z_ref, y_ref, k_ref, v_ref, own_ref, sent_ref):
    groups, _, count, _ = sent_ref.shape
    here = pl.ds(pl.multiple_of(z_ref[0] * HEAD_SIZE, HEAD_SIZE), HEAD_SIZE)
    own_ref[0] = k_ref[:, here]
    own_ref[1] = v_ref[:, here]
    rows = pl.ds(pl.multiple_of(y_ref[0] * count, count), count)
    for group in range(groups):
        columns = slice(group * HEAD_SIZE, (group + 1) * HEAD_SIZE)
        sent_ref[group, 0] = k_ref[rows, columns]
        sent_ref[group, 1] = v_ref[rows, columns]


def pack(z, y, y_size, keys, values):
    groups = keys.shape[1] // HEAD_SIZE
    count = keys.shape[0]
    out_shape = [
        jax.ShapeDtypeStruct((2, count, HEAD_SIZE), BF16),
        jax.ShapeDtypeStruct((groups, 2, count // y_size, HEAD_SIZE), BF16),
    ]
    return call(
        pack_kernel,
        "pack_heads",
        2,
        grid=(1,),
        in_specs=[SMEM] * 2 + [whole(keys), whole(values)],
        out_specs=[whole(s) for s in out_shape],
        out_shape=out_shape,
    )(z.reshape(1), y.reshape(1), keys, values)


def unpack_kernel(z_ref, got_ref, out_ref):
    groups, _, count, _ = got_ref.shape
    for i in range(groups - 1):
        source = lax.rem(z_ref[0] + 1 + i, groups)
        out_ref[0, i * count : (i + 1) * count] = got_ref[source, 0]
        out_ref[1, i * count : (i + 1) * count] = got_ref[source, 1]


def unpack(z, got, order):
    groups, two, count, width = got.shape
    out = jax.ShapeDtypeStruct((two, (groups - 1) * count, width), BF16)
    return call(
        unpack_kernel,
        "unpack_heads",
        1,
        order,
        grid=(1,),
        in_specs=[SMEM, whole(got)],
        out_specs=whole(out),
        out_shape=out,
    )(z.reshape(1), got)


def after(array, *others):
    return lax.optimization_barrier((array, *others))[0]


def weight_of_core(out_weight, c):
    depth, width = out_weight.shape
    quarters = out_weight.T.reshape(2, 2, width // 4, depth)
    of_c = lax.dynamic_index_in_dim(quarters, c, 1, keepdims=False)
    sent = lax.dynamic_index_in_dim(quarters, 1 - c, 1, keepdims=False)
    return jnp.concatenate([of_c, lax.ppermute(sent, "c", SWAP)], axis=2)


def on_device(queries, keys, values, resp_keys, resp_values, lengths, out_weight):
    xh, y, z, xl, c = (lax.axis_index(a) for a in SUB_AXES)
    resp_count, resp_len, features = queries.shape
    tokens = resp_count * resp_len
    y_size = lax.axis_size("y")
    own_heads = features // HEAD_SIZE
    part_tokens = tokens // PARTS
    slot_rows = own_heads * part_tokens
    width = out_weight.shape[1]

    both = weight_of_core(out_weight, c)
    w_own = lax.dynamic_index_in_dim(both, xl, 0, keepdims=False)
    w_sent = lax.dynamic_index_in_dim(both, 1 - xl, 0, keepdims=False)
    w_x = lax.ppermute(w_sent, "xl", SWAP)
    w_h = lax.ppermute(w_own, "xh", SWAP)
    w_xh = lax.ppermute(w_sent, ("xh", "xl"), [(i, 3 - i) for i in range(4)])
    own_block, sent = pack(z, y, y_size, keys, values)
    got = lax.all_to_all(after(sent, both), "z", split_axis=0, concat_axis=0, tiled=True)

    q_own = after(queries, own_block).reshape(-1, PARTS, SLAB, own_heads, HEAD_SIZE)
    q_own = q_own.transpose(1, 3, 0, 2, 4).reshape(PARTS * slot_rows, HEAD_SIZE)
    q_every = lax.all_gather(q_own, ("xl", "c"), axis=0, tiled=False)

    up = [(i, (i + 1) % y_size) for i in range(y_size)]
    down = [(i, (i - 1) % y_size) for i in range(y_size)]
    head = z * HEAD_SIZE
    rk = lax.dynamic_slice_in_dim(resp_keys, head, HEAD_SIZE, 2)
    rv = lax.dynamic_slice_in_dim(resp_values, head, HEAD_SIZE, 2)
    state = first_own(q_own, rk, rv, own_block, ())
    near_y = unpack(z, after(got, state[0]), (w_x, w_h, w_xh))
    from_below = lax.ppermute(near_y, "y", up)
    from_above = lax.ppermute(near_y, "y", down)
    here = jnp.concatenate([w_own, w_x], axis=1)
    there = jnp.concatenate([w_h, w_xh], axis=1)
    weight = lax.all_gather(jnp.concatenate([here, there], axis=0), "y", axis=0, tiled=True)

    q_every = after(q_every, state[0])
    mine = 2 * xl + c
    slots = [q_own] + [
        lax.dynamic_index_in_dim(q_every, mine ^ i, 0, keepdims=False) for i in (2, 1, 3)
    ]
    slots = [q.reshape(PARTS, 1, slot_rows, HEAD_SIZE) for q in slots]
    q_all = jnp.concatenate(slots, axis=1).reshape(-1, HEAD_SIZE)
    state = first_all(q_all, own_block, near_y, state, 1024, ())
    far_k = lax.ppermute(after(from_below, state[0])[0], "y", up)
    far_v = lax.ppermute(after(from_above, state[0])[1], "y", down)
    state = attend_more(q_all, [from_below, from_above], state, 1024, ())
    half = 2 * slot_rows
    blocks = [far_k, far_v]
    far = []
    for part in range(PARTS):
        order = (far[-1],) if far else ()
        far.append(attend_far(q_all, blocks, state, part, half, order))
    far_c = [lax.ppermute(f, "c", SWAP) for f in far]
    near, near_x, merged = [], [], []
    for part in range(PARTS):
        order = (near[-1][0],) if near else (far[-1],)
        out, lines, sent = attend_near(q_all, blocks, state, far_c[part], part, half, order)
        near.append((out, lines))
        near_x.append(lax.ppermute(sent, "xl", SWAP))
    for part in range(PARTS - 1):
        merged.append(
            last_merge(part, lengths, *near[part], near_x[part], part_tokens, (near[-1][0], weight))
        )
    merged.append(
        last_merge(PARTS - 1, lengths, *near[-1], near_x[-1], part_tokens, (merged[-1],))
    )
    pairs = []
    for attended in merged:
        pairs += [attended, lax.ppermute(attended, "c", SWAP)]
    partial = project(pairs, weight)
    partial = partial.reshape(partial.shape[0], PARTS * SLAB, partial.shape[-1])
    received = lax.all_to_all(partial, PREFIX, split_axis=0, concat_axis=0, tiled=True)
    blocks = 2 * y_size
    return add_up(xh, [received], width * blocks, blocks)


def solution(mesh):
    shape = (2, mesh.shape["batch"] // 2, mesh.shape["prefix"] // 4, 2, 2)
    fine = Mesh(mesh.devices.reshape(shape), SUB_AXES)
    batch = ("xh", "y")
    placed = (
        P(batch, None, PREFIX),
        P(PREFIX, None),
        P(PREFIX, None),
        P(batch, None, None),
        P(batch, None, None),
        P(batch),
        P(PREFIX, batch),
    )
    return jax.shard_map(
        on_device,
        mesh=fine,
        in_specs=placed,
        out_specs=P(batch + PREFIX, None),
        check_vma=False,
    )
```

```python
import functools
import math

import jax
import jax.numpy as jnp
from jax import lax
from jax.experimental import pallas as pl
from jax.experimental.pallas import tpu as pltpu
from jax.sharding import Mesh, PartitionSpec as P

HEAD_SIZE = 128
LANES = 128
F32 = jnp.float32
BF16 = jnp.bfloat16
SCORE_SCALE = HEAD_SIZE**-0.5 * math.log2(math.e)
LOWEST = -1e30
VMEM_LIMIT = 24 * 2**20
SUB_AXES = ("xh", "y", "z", "xl", "c")
PREFIX = ("z", "xl", "c")
SWAP = [(0, 1), (1, 0)]
PARTS = 2
SLAB = 8
SLOTS = 4
STAT_ROWS = 16
CHUNK = 256
FLOPS_PER_MICRO = 1.15e9


def score_dot(q, k):
    return lax.dot_general(q, k, (((1,), (1,)), ((), ())), preferred_element_type=F32)


def absorb(state, scores, values):
    top, total, acc = state
    new_top = jnp.maximum(top, scores.max(-1, keepdims=True) * SCORE_SCALE)
    decay = jnp.exp2(top - new_top)
    weights = jnp.exp2(scores * SCORE_SCALE - new_top).astype(BF16)
    extended = jnp.concatenate([values, jnp.ones(values.shape, BF16)], axis=1)
    added = jnp.dot(weights, extended, preferred_element_type=F32)
    return new_top, total * decay + added[:, 128:129], acc * decay + added[:, :128]


def empty_state(rows):
    return (
        jnp.full((rows, 1), LOWEST, F32),
        jnp.zeros((rows, 1), F32),
        jnp.zeros((rows, HEAD_SIZE), F32),
    )


def store_state(state, acc_out, stat_out):
    top, total, acc = state
    acc_out[...] = acc
    lane = lax.broadcasted_iota(jnp.int32, acc.shape, 1)
    stat_out[...] = jnp.where(lane < 64, top, total)


def load_state(acc_in, stat_in):
    stat = stat_in[...]
    lane = lax.broadcasted_iota(jnp.int32, stat.shape, 1)
    top = jnp.where(lane < 64, stat, LOWEST).max(-1, keepdims=True)
    total = jnp.where(lane < 64, 0.0, stat).max(-1, keepdims=True)
    return top, total, acc_in[...]


def rows_of(pieces):
    parts = [ref[at:to, :] for ref, at, to in pieces]
    return parts[0] if len(parts) == 1 else jnp.concatenate(parts, axis=0)


def absorb_blocks(state, q, blocks, chunk=CHUNK):
    sizes = [keys.shape[0] for keys, _ in blocks]
    ends = [sum(sizes[: i + 1]) for i in range(len(sizes))]
    at = 0
    while at < ends[-1]:
        to = min(at + chunk, ends[-1])
        spans = []
        for (keys, values), end, size in zip(blocks, ends, sizes):
            low, high = max(at, end - size), min(to, end)
            if low < high:
                spans.append((keys, values, low - end + size, high - end + size))
        keys = rows_of([(k, low, high) for k, _, low, high in spans])
        values = rows_of([(v, low, high) for _, v, low, high in spans])
        state = absorb(state, score_dot(q, keys), values)
        at = to
    return state


def first_rows(block):
    cut = block.shape[1] // CHUNK * CHUNK
    return block.at[0, :cut, :], block.at[1, :cut, :]


def other_rows(block):
    cut = block.shape[1] // CHUNK * CHUNK
    return block.at[0, cut:, :], block.at[1, cut:, :]


def absorb_block(state, q, keys, values, chunk=CHUNK):
    return absorb_blocks(state, q, [(keys, values)], chunk)


def first_own_kernel(q_ref, rk_ref, rv_ref, block, acc_out, stat_out):
    count, resp_len, _ = rk_ref.shape
    part = resp_len // PARTS
    row = lax.broadcasted_iota(jnp.int32, (part, resp_len), 0)
    col = lax.broadcasted_iota(jnp.int32, (part, resp_len), 1)
    token = (row // SLAB) * (PARTS * SLAB) + pl.program_id(0) * SLAB + row % SLAB
    tops, totals, accs = [], [], []
    for at in range(0, q_ref.shape[0], part):
        r = at // part % count
        scores = score_dot(q_ref[at : at + part, :], rk_ref[r])
        scores = jnp.where(token >= col, scores, LOWEST)
        top, total, acc = absorb(empty_state(part), scores, rv_ref[r])
        tops.append(top)
        totals.append(total)
        accs.append(acc)
    state = tuple(jnp.concatenate(part, axis=0) for part in (tops, totals, accs))
    state = absorb_block(state, q_ref[...], block.at[0], block.at[1], 512)
    store_state(state, acc_out, stat_out)


def first_all_kernel(q_ref, block, near_block, acc_in, stat_in, acc_out, stat_out):
    rows = q_ref.shape[0]
    own_rows = acc_in.shape[0]
    own = pl.program_id(0) % (SLOTS * own_rows // rows) == 0

    def absorb_first(start):
        state = empty_state(rows - start)
        state = absorb_block(state, q_ref[start:, :], block.at[0], block.at[1])
        store_state(state, acc_out.at[start:, :], stat_out.at[start:, :])

    @pl.when(own)
    def _():
        acc_out[:own_rows, :] = acc_in[...]
        stat_out[:own_rows, :] = stat_in[...]
        absorb_first(own_rows)

    @pl.when(jnp.logical_not(own))
    def _():
        absorb_first(0)

    state = load_state(acc_out, stat_out)
    state = absorb_blocks(state, q_ref[...], [first_rows(near_block)])
    store_state(state, acc_out, stat_out)


def middle_kernel(count, q_ref, *refs):
    blocks, (acc_in, stat_in, acc_out, stat_out) = refs[:count], refs[count:]
    state = load_state(acc_in, stat_in)
    near, below, above = blocks
    pairs = [other_rows(near), (below.at[0], below.at[1]), first_rows(above)]
    state = absorb_blocks(state, q_ref[...], pairs)
    store_state(state, acc_out, stat_out)


def narrow(columns):
    rows = columns.shape[0]
    lines = []
    for at in range(0, rows, LANES):
        wide = jnp.broadcast_to(columns[at : at + LANES], (LANES, LANES))
        lines.append(wide.T[0:1])
    lines.append(jnp.zeros((STAT_ROWS - rows // LANES, LANES), F32))
    return jnp.concatenate(lines, axis=0)


def widen(lines, rows):
    columns = []
    for i in range(rows // LANES):
        columns.append(jnp.broadcast_to(lines[i : i + 1], (LANES, LANES)).T)
    return jnp.concatenate(columns, axis=0)


def store_sent(sent_ref, out, lines):
    rows = out.shape[0]
    sent_ref[0:rows, :] = out.astype(BF16)
    for i in range(3):
        term = lines.astype(BF16)
        sent_ref[rows + i * STAT_ROWS : rows + (i + 1) * STAT_ROWS, :] = term
        lines = lines - term.astype(F32)


def load_sent(sent_ref):
    rows = sent_ref.shape[0] - 3 * STAT_ROWS
    lines = jnp.zeros((STAT_ROWS, LANES), F32)
    for i in range(3):
        term = sent_ref[rows + i * STAT_ROWS : rows + (i + 1) * STAT_ROWS, :]
        lines = lines + term.astype(F32)
    return sent_ref[0:rows, :].astype(F32), widen(lines, rows)


def merge(out_a, lse_a, out_b, lse_b):
    top = jnp.maximum(lse_a, lse_b)
    weight_a, weight_b = jnp.exp2(lse_a - top), jnp.exp2(lse_b - top)
    total = weight_a + weight_b
    return (weight_a * out_a + weight_b * out_b) / total, top + jnp.log2(total)


def finish(q_ref, blocks, acc_in, stat_in):
    state = load_state(acc_in, stat_in)
    above, keys, values = blocks
    pairs = [other_rows(above), (keys, values)]
    top, total, acc = absorb_blocks(state, q_ref[...], pairs)
    return acc / total, top + jnp.log2(total)


def far_kernel(q_ref, acc_in, stat_in, *refs):
    blocks, sent_ref = refs[:-1], refs[-1]
    out, lse = finish(q_ref, blocks, acc_in, stat_in)
    store_sent(sent_ref, out, narrow(lse))


def near_kernel(q_ref, acc_in, stat_in, *refs):
    blocks, (got_ref, out_ref, lines_ref, sent_ref) = refs[:-4], refs[-4:]
    out, lse = finish(q_ref, blocks, acc_in, stat_in)
    out, lse = merge(out, jnp.broadcast_to(lse, out.shape), *load_sent(got_ref))
    lines = narrow(lse[:, 0:1])
    out_ref[...] = out
    lines_ref[...] = lines
    store_sent(sent_ref, out, lines)


def last_merge_kernel(part, lengths_ref, out_ref, lines_ref, got_ref, attended_ref):
    tokens, width = attended_ref.shape
    rows = out_ref.shape[0]
    half = rows // 2
    got, got_lse = load_sent(got_ref)
    got = jnp.concatenate([got[half:], got[:half]], axis=0)
    got_lse = jnp.concatenate([got_lse[half:], got_lse[:half]], axis=0)
    out, _ = merge(out_ref[...], widen(lines_ref[...], rows), got, got_lse)
    row = lax.broadcasted_iota(jnp.int32, (tokens, LANES), 0)
    count = lengths_ref.shape[0]
    per = tokens // count
    token = (row % per) // SLAB * (PARTS * SLAB) + part * SLAB + row % SLAB
    valid = jnp.zeros((tokens, LANES), jnp.int32)
    for r in range(count):
        valid = jnp.where(row // per == r, lengths_ref[r], valid)
    live = token < valid
    for i in range(width // HEAD_SIZE):
        head = jnp.where(live, out[i * tokens : (i + 1) * tokens], 0.0)
        attended_ref[:, i * HEAD_SIZE : (i + 1) * HEAD_SIZE] = head.astype(BF16)


def project_kernel(w_ref, *refs):
    pairs, out_ref = refs[:-1], refs[-1]
    devices, _, rows, width = out_ref.shape
    depth = w_ref.shape[1] // 4
    for part in range(PARTS):
        product = 0.0
        for i in range(4):
            ref, at = pairs[2 * part + i % 2], i // 2 * depth
            weight = w_ref[:, i * depth : (i + 1) * depth]
            product = product + score_dot(ref[:, at : at + depth], weight)
        out_ref[:, part] = product.reshape(devices, rows, width).astype(BF16)


def total_kernel(blocks, xh_ref, *refs):
    parts, out_ref = refs[:-1], refs[-1]
    half = out_ref.shape[1] // 2
    lines = []
    for ref in parts:
        count, rows, columns = ref.shape
        sums = ref[...].astype(F32).reshape(count // SLOTS, SLOTS, rows, columns).sum(0)
        piece = columns // blocks
        turned = []
        for rel in range(2):
            starts = range(rel * piece, columns, 2 * piece)
            pieces = [sums[q][:, at : at + piece] for at in starts for q in range(SLOTS)]
            turned.append(jnp.concatenate(pieces, axis=1))
        lines.append(turned)
    here = jnp.concatenate([line[0] for line in lines], axis=0).astype(BF16)
    there = jnp.concatenate([line[1] for line in lines], axis=0).astype(BF16)
    at_here = pl.multiple_of(xh_ref[0] * half, half)
    at_there = pl.multiple_of((1 - xh_ref[0]) * half, half)
    out_ref[:, pl.ds(at_here, half)] = here
    out_ref[:, pl.ds(at_there, half)] = there


def call(kernel, name, micros, order=(), in_specs=(), **options):
    def run(*operands):
        held = jnp.zeros((1,), jnp.int32)
        if order:
            held = after(held, *order)
        return pl.pallas_call(
            lambda held_ref, *refs: kernel(*refs),
            name=name,
            in_specs=[SMEM, *in_specs],
            cost_estimate=pl.CostEstimate(
                flops=int(micros * FLOPS_PER_MICRO), bytes_accessed=1, transcendentals=0
            ),
            compiler_params=pltpu.CompilerParams(vmem_limit_bytes=VMEM_LIMIT),
            **options,
        )(held, *operands)

    return run


def whole(array):
    return pl.BlockSpec(array.shape, lambda i: (0,) * array.ndim)


def rows_spec(tile, index=lambda i: i):
    return pl.BlockSpec((tile, HEAD_SIZE), lambda i: (index(i), 0))


def shapes_of(arrays):
    return [jax.ShapeDtypeStruct(a.shape, a.dtype) for a in arrays]


VMEM = pl.BlockSpec(memory_space=pltpu.VMEM)
SMEM = pl.BlockSpec(memory_space=pltpu.SMEM)


def first_own(q, resp_k, resp_v, block, order):
    tile = q.shape[0] // PARTS
    state = jax.ShapeDtypeStruct(q.shape, F32)
    return call(
        first_own_kernel,
        "attend_own",
        5,
        order,
        grid=(PARTS,),
        in_specs=[rows_spec(tile), whole(resp_k), whole(resp_v), whole(block)],
        out_specs=[rows_spec(tile)] * 2,
        out_shape=[state] * 2,
    )(q, resp_k, resp_v, block)


def first_all(q, block, near_block, own_state, tile, order):
    own_rows = q.shape[0] // (PARTS * SLOTS)
    state = jax.ShapeDtypeStruct(q.shape, F32)
    tiles = q.shape[0] // tile
    held = rows_spec(own_rows, lambda i: i * PARTS // tiles)
    return call(
        first_all_kernel,
        "attend_first",
        11,
        order,
        grid=(tiles,),
        in_specs=[rows_spec(tile), whole(block), whole(near_block), held, held],
        out_specs=[rows_spec(tile)] * 2,
        out_shape=[state] * 2,
    )(q, block, near_block, *own_state)


def attend_more(q, blocks, state, tile, order, start=0, rows=None):
    rows = rows or q.shape[0]
    count = len(blocks)
    at = start // tile
    moved = rows_spec(tile, lambda i: i + at)
    return call(
        functools.partial(middle_kernel, count),
        "attend_more",
        7 * count * rows // q.shape[0],
        order,
        grid=(rows // tile,),
        in_specs=[moved] + [whole(b) for b in blocks] + [moved] * 2,
        out_specs=[rows_spec(tile)] * 2,
        out_shape=[jax.ShapeDtypeStruct((rows, HEAD_SIZE), F32)] * 2,
    )(q, *blocks, *state)


def attend_far(q, blocks, state, part, rows, order):
    moved = rows_spec(rows, lambda i: 2 * part + 1)
    sent = jax.ShapeDtypeStruct((rows + 3 * STAT_ROWS, HEAD_SIZE), BF16)
    return call(
        far_kernel,
        "attend_far",
        2,
        order,
        grid=(1,),
        in_specs=[moved] * 3 + [whole(b) for b in blocks],
        out_specs=whole(sent),
        out_shape=sent,
    )(q, *state, *blocks)


def attend_near(q, blocks, state, got, part, rows, order):
    moved = rows_spec(rows, lambda i: 2 * part)
    out_shape = [
        jax.ShapeDtypeStruct((rows, HEAD_SIZE), F32),
        jax.ShapeDtypeStruct((STAT_ROWS, LANES), F32),
        jax.ShapeDtypeStruct(got.shape, BF16),
    ]
    return call(
        near_kernel,
        "attend_near",
        2,
        order,
        grid=(1,),
        in_specs=[moved] * 3 + [whole(b) for b in blocks] + [whole(got)],
        out_specs=[whole(s) for s in out_shape],
        out_shape=out_shape,
    )(q, *state, *blocks, got)


def last_merge(part, lengths, out, lines, got, tokens, order):
    attended = jax.ShapeDtypeStruct((tokens, out.shape[0] // tokens * HEAD_SIZE), BF16)
    return call(
        functools.partial(last_merge_kernel, part),
        "merge_last",
        1,
        order,
        grid=(1,),
        in_specs=[SMEM] + [whole(a) for a in (out, lines, got)],
        out_specs=whole(attended),
        out_shape=attended,
    )(lengths, out, lines, got)


def project(pairs, weight, tile=640):
    devices = pairs[0].shape[0] // SLAB
    columns, depth = weight.shape
    return call(
        project_kernel,
        "project",
        3,
        grid=(columns // tile,),
        in_specs=[pl.BlockSpec((tile, depth), lambda i: (i, 0))] + [whole(a) for a in pairs],
        out_specs=pl.BlockSpec((devices, PARTS, SLAB, tile), lambda i: (0, 0, 0, i)),
        out_shape=jax.ShapeDtypeStruct((devices, PARTS, SLAB, columns), BF16),
    )(weight, *pairs)


def add_up(xh, parts, width, blocks):
    rows = sum(part.shape[1] for part in parts)
    out = jax.ShapeDtypeStruct((rows, width), BF16)
    return call(
        functools.partial(total_kernel, blocks),
        "add_up",
        2,
        grid=(1,),
        in_specs=[SMEM] + [whole(p) for p in parts],
        out_specs=whole(out),
        out_shape=out,
    )(xh.reshape(1), *parts)


def pack_kernel(z_ref, y_ref, k_ref, v_ref, own_ref, sent_ref):
    groups, _, count, _ = sent_ref.shape
    here = pl.ds(pl.multiple_of(z_ref[0] * HEAD_SIZE, HEAD_SIZE), HEAD_SIZE)
    own_ref[0] = k_ref[:, here]
    own_ref[1] = v_ref[:, here]
    rows = pl.ds(pl.multiple_of(y_ref[0] * count, count), count)
    for group in range(groups):
        columns = slice(group * HEAD_SIZE, (group + 1) * HEAD_SIZE)
        sent_ref[group, 0] = k_ref[rows, columns]
        sent_ref[group, 1] = v_ref[rows, columns]


def pack(z, y, y_size, keys, values):
    groups = keys.shape[1] // HEAD_SIZE
    count = keys.shape[0]
    out_shape = [
        jax.ShapeDtypeStruct((2, count, HEAD_SIZE), BF16),
        jax.ShapeDtypeStruct((groups, 2, count // y_size, HEAD_SIZE), BF16),
    ]
    return call(
        pack_kernel,
        "pack_heads",
        2,
        grid=(1,),
        in_specs=[SMEM] * 2 + [whole(keys), whole(values)],
        out_specs=[whole(s) for s in out_shape],
        out_shape=out_shape,
    )(z.reshape(1), y.reshape(1), keys, values)


def unpack_kernel(z_ref, got_ref, out_ref):
    groups, _, count, _ = got_ref.shape
    for i in range(groups - 1):
        source = lax.rem(z_ref[0] + 1 + i, groups)
        out_ref[0, i * count : (i + 1) * count] = got_ref[source, 0]
        out_ref[1, i * count : (i + 1) * count] = got_ref[source, 1]


def unpack(z, got, order):
    groups, two, count, width = got.shape
    out = jax.ShapeDtypeStruct((two, (groups - 1) * count, width), BF16)
    return call(
        unpack_kernel,
        "unpack_heads",
        1,
        order,
        grid=(1,),
        in_specs=[SMEM, whole(got)],
        out_specs=whole(out),
        out_shape=out,
    )(z.reshape(1), got)


def after(array, *others):
    return lax.optimization_barrier((array, *others))[0]


def weight_of_core(out_weight, c):
    depth, width = out_weight.shape
    quarters = out_weight.T.reshape(2, 2, width // 4, depth)
    of_c = lax.dynamic_index_in_dim(quarters, c, 1, keepdims=False)
    sent = lax.dynamic_index_in_dim(quarters, 1 - c, 1, keepdims=False)
    return jnp.concatenate([of_c, lax.ppermute(sent, "c", SWAP)], axis=2)


def on_device(queries, keys, values, resp_keys, resp_values, lengths, out_weight):
    xh, y, z, xl, c = (lax.axis_index(a) for a in SUB_AXES)
    resp_count, resp_len, features = queries.shape
    tokens = resp_count * resp_len
    y_size = lax.axis_size("y")
    own_heads = features // HEAD_SIZE
    part_tokens = tokens // PARTS
    slot_rows = own_heads * part_tokens
    width = out_weight.shape[1]

    both = weight_of_core(out_weight, c)
    w_own = lax.dynamic_index_in_dim(both, xl, 0, keepdims=False)
    w_sent = lax.dynamic_index_in_dim(both, 1 - xl, 0, keepdims=False)
    w_x = lax.ppermute(w_sent, "xl", SWAP)
    w_h = lax.ppermute(w_own, "xh", SWAP)
    w_xh = lax.ppermute(w_sent, ("xh", "xl"), [(i, 3 - i) for i in range(4)])
    own_block, sent = pack(z, y, y_size, keys, values)
    got = lax.all_to_all(after(sent, both), "z", split_axis=0, concat_axis=0, tiled=True)

    q_own = after(queries, own_block).reshape(-1, PARTS, SLAB, own_heads, HEAD_SIZE)
    q_own = q_own.transpose(1, 3, 0, 2, 4).reshape(PARTS * slot_rows, HEAD_SIZE)
    q_every = lax.all_gather(q_own, ("xl", "c"), axis=0, tiled=False)

    up = [(i, (i + 1) % y_size) for i in range(y_size)]
    down = [(i, (i - 1) % y_size) for i in range(y_size)]
    head = z * HEAD_SIZE
    rk = lax.dynamic_slice_in_dim(resp_keys, head, HEAD_SIZE, 2)
    rv = lax.dynamic_slice_in_dim(resp_values, head, HEAD_SIZE, 2)
    state = first_own(q_own, rk, rv, own_block, ())
    near_y = unpack(z, after(got, state[0]), (w_x, w_h, w_xh))
    from_below = lax.ppermute(near_y, "y", up)
    from_above = lax.ppermute(near_y, "y", down)
    here = jnp.concatenate([w_own, w_x], axis=1)
    there = jnp.concatenate([w_h, w_xh], axis=1)
    weight = lax.all_gather(jnp.concatenate([here, there], axis=0), "y", axis=0, tiled=True)

    q_every = after(q_every, state[0])
    mine = 2 * xl + c
    slots = [q_own] + [
        lax.dynamic_index_in_dim(q_every, mine ^ i, 0, keepdims=False) for i in (2, 1, 3)
    ]
    slots = [q.reshape(PARTS, 1, slot_rows, HEAD_SIZE) for q in slots]
    q_all = jnp.concatenate(slots, axis=1).reshape(-1, HEAD_SIZE)
    state = first_all(q_all, own_block, near_y, state, 1024, ())
    far_k = lax.ppermute(after(from_below, state[0])[0], "y", up)
    far_v = lax.ppermute(after(from_above, state[0])[1], "y", down)
    state = attend_more(q_all, [near_y, from_below, from_above], state, 1024, ())
    half = 2 * slot_rows
    blocks = [from_above, far_k, far_v]
    far = []
    for part in range(PARTS):
        order = (far[-1],) if far else ()
        far.append(attend_far(q_all, blocks, state, part, half, order))
    far_c = [lax.ppermute(f, "c", SWAP) for f in far]
    near, near_x, merged = [], [], []
    for part in range(PARTS):
        order = (near[-1][0],) if near else (far[-1],)
        out, lines, sent = attend_near(q_all, blocks, state, far_c[part], part, half, order)
        near.append((out, lines))
        near_x.append(lax.ppermute(sent, "xl", SWAP))
    for part in range(PARTS - 1):
        merged.append(
            last_merge(part, lengths, *near[part], near_x[part], part_tokens, (near[-1][0], weight))
        )
    merged.append(
        last_merge(PARTS - 1, lengths, *near[-1], near_x[-1], part_tokens, (merged[-1],))
    )
    pairs = []
    for attended in merged:
        pairs += [attended, lax.ppermute(attended, "c", SWAP)]
    partial = project(pairs, weight)
    partial = partial.reshape(partial.shape[0], PARTS * SLAB, partial.shape[-1])
    received = lax.all_to_all(partial, PREFIX, split_axis=0, concat_axis=0, tiled=True)
    blocks = 2 * y_size
    return add_up(xh, [received], width * blocks, blocks)


def solution(mesh):
    shape = (2, mesh.shape["batch"] // 2, mesh.shape["prefix"] // 4, 2, 2)
    fine = Mesh(mesh.devices.reshape(shape), SUB_AXES)
    batch = ("xh", "y")
    placed = (
        P(batch, None, PREFIX),
        P(PREFIX, None),
        P(PREFIX, None),
        P(batch, None, None),
        P(batch, None, None),
        P(batch),
        P(PREFIX, batch),
    )
    return jax.shard_map(
        on_device,
        mesh=fine,
        in_specs=placed,
        out_specs=P(batch + PREFIX, None),
        check_vma=False,
    )
```

```python
import functools
import math

import jax
import jax.numpy as jnp
from jax import lax
from jax.experimental import pallas as pl
from jax.experimental.pallas import tpu as pltpu
from jax.sharding import Mesh, PartitionSpec as P

HEAD_SIZE = 128
LANES = 128
F32 = jnp.float32
BF16 = jnp.bfloat16
SCORE_SCALE = HEAD_SIZE**-0.5 * math.log2(math.e)
LOWEST = -1e30
VMEM_LIMIT = 24 * 2**20
SUB_AXES = ("xh", "y", "z", "xl", "c")
PREFIX = ("z", "xl", "c")
SWAP = [(0, 1), (1, 0)]
PARTS = 2
SLAB = 8
SLOTS = 4
STAT_ROWS = 16
CHUNK = 256
FLOPS_PER_MICRO = 1.15e9


def score_dot(q, k):
    return lax.dot_general(q, k, (((1,), (1,)), ((), ())), preferred_element_type=F32)


def absorb(state, scores, values):
    top, total, acc = state
    new_top = jnp.maximum(top, scores.max(-1, keepdims=True) * SCORE_SCALE)
    decay = jnp.exp2(top - new_top)
    weights = jnp.exp2(scores * SCORE_SCALE - new_top).astype(BF16)
    extended = jnp.concatenate([values, jnp.ones(values.shape, BF16)], axis=1)
    added = jnp.dot(weights, extended, preferred_element_type=F32)
    return new_top, total * decay + added[:, 128:129], acc * decay + added[:, :128]


def empty_state(rows):
    return (
        jnp.full((rows, 1), LOWEST, F32),
        jnp.zeros((rows, 1), F32),
        jnp.zeros((rows, HEAD_SIZE), F32),
    )


def store_state(state, acc_out, stat_out):
    top, total, acc = state
    acc_out[...] = acc
    lane = lax.broadcasted_iota(jnp.int32, acc.shape, 1)
    stat_out[...] = jnp.where(lane < 64, top, total)


def load_state(acc_in, stat_in):
    stat = stat_in[...]
    lane = lax.broadcasted_iota(jnp.int32, stat.shape, 1)
    top = jnp.where(lane < 64, stat, LOWEST).max(-1, keepdims=True)
    total = jnp.where(lane < 64, 0.0, stat).max(-1, keepdims=True)
    return top, total, acc_in[...]


def rows_of(pieces):
    parts = [ref[at:to, :] for ref, at, to in pieces]
    return parts[0] if len(parts) == 1 else jnp.concatenate(parts, axis=0)


def absorb_blocks(state, q, blocks, chunk=CHUNK):
    sizes = [keys.shape[0] for keys, _ in blocks]
    ends = [sum(sizes[: i + 1]) for i in range(len(sizes))]
    at = 0
    while at < ends[-1]:
        to = min(at + chunk, ends[-1])
        spans = []
        for (keys, values), end, size in zip(blocks, ends, sizes):
            low, high = max(at, end - size), min(to, end)
            if low < high:
                spans.append((keys, values, low - end + size, high - end + size))
        keys = rows_of([(k, low, high) for k, _, low, high in spans])
        values = rows_of([(v, low, high) for _, v, low, high in spans])
        state = absorb(state, score_dot(q, keys), values)
        at = to
    return state


def first_rows(block):
    cut = block.shape[1] // CHUNK * CHUNK
    return block.at[0, :cut, :], block.at[1, :cut, :]


def other_rows(block):
    cut = block.shape[1] // CHUNK * CHUNK
    return block.at[0, cut:, :], block.at[1, cut:, :]


def absorb_block(state, q, keys, values, chunk=CHUNK):
    return absorb_blocks(state, q, [(keys, values)], chunk)


def first_own_kernel(q_ref, rk_ref, rv_ref, block, acc_out, stat_out):
    count, resp_len, _ = rk_ref.shape
    part = resp_len // PARTS
    row = lax.broadcasted_iota(jnp.int32, (part, resp_len), 0)
    col = lax.broadcasted_iota(jnp.int32, (part, resp_len), 1)
    token = (row // SLAB) * (PARTS * SLAB) + pl.program_id(0) * SLAB + row % SLAB
    tops, totals, accs = [], [], []
    for at in range(0, q_ref.shape[0], part):
        r = at // part % count
        scores = score_dot(q_ref[at : at + part, :], rk_ref[r])
        scores = jnp.where(token >= col, scores, LOWEST)
        top, total, acc = absorb(empty_state(part), scores, rv_ref[r])
        tops.append(top)
        totals.append(total)
        accs.append(acc)
    state = tuple(jnp.concatenate(part, axis=0) for part in (tops, totals, accs))
    state = absorb_block(state, q_ref[...], block.at[0], block.at[1], 512)
    store_state(state, acc_out, stat_out)


def first_all_kernel(q_ref, block, near_block, acc_in, stat_in, acc_out, stat_out):
    rows = q_ref.shape[0]
    own_rows = acc_in.shape[0]
    own = pl.program_id(0) % (SLOTS * own_rows // rows) == 0

    def absorb_first(start):
        state = empty_state(rows - start)
        state = absorb_block(state, q_ref[start:, :], block.at[0], block.at[1])
        store_state(state, acc_out.at[start:, :], stat_out.at[start:, :])

    @pl.when(own)
    def _():
        acc_out[:own_rows, :] = acc_in[...]
        stat_out[:own_rows, :] = stat_in[...]
        absorb_first(own_rows)

    @pl.when(jnp.logical_not(own))
    def _():
        absorb_first(0)

    state = load_state(acc_out, stat_out)
    state = absorb_blocks(state, q_ref[...], [first_rows(near_block)])
    store_state(state, acc_out, stat_out)


def middle_kernel(count, q_ref, *refs):
    blocks, (acc_in, stat_in, acc_out, stat_out) = refs[:count], refs[count:]
    state = load_state(acc_in, stat_in)
    near, below, above = blocks
    pairs = [other_rows(near), (below.at[0], below.at[1]), first_rows(above)]
    state = absorb_blocks(state, q_ref[...], pairs)
    store_state(state, acc_out, stat_out)


def narrow(columns):
    rows = columns.shape[0]
    lines = []
    for at in range(0, rows, LANES):
        wide = jnp.broadcast_to(columns[at : at + LANES], (LANES, LANES))
        lines.append(wide.T[0:1])
    lines.append(jnp.zeros((STAT_ROWS - rows // LANES, LANES), F32))
    return jnp.concatenate(lines, axis=0)


def widen(lines, rows):
    columns = []
    for i in range(rows // LANES):
        columns.append(jnp.broadcast_to(lines[i : i + 1], (LANES, LANES)).T)
    return jnp.concatenate(columns, axis=0)


def store_sent(sent_ref, out, lines):
    rows = out.shape[0]
    sent_ref[0:rows, :] = out.astype(BF16)
    for i in range(3):
        term = lines.astype(BF16)
        sent_ref[rows + i * STAT_ROWS : rows + (i + 1) * STAT_ROWS, :] = term
        lines = lines - term.astype(F32)


def load_sent(sent_ref):
    rows = sent_ref.shape[0] - 3 * STAT_ROWS
    lines = jnp.zeros((STAT_ROWS, LANES), F32)
    for i in range(3):
        term = sent_ref[rows + i * STAT_ROWS : rows + (i + 1) * STAT_ROWS, :]
        lines = lines + term.astype(F32)
    return sent_ref[0:rows, :].astype(F32), widen(lines, rows)


def merge(out_a, lse_a, out_b, lse_b):
    top = jnp.maximum(lse_a, lse_b)
    weight_a, weight_b = jnp.exp2(lse_a - top), jnp.exp2(lse_b - top)
    total = weight_a + weight_b
    return (weight_a * out_a + weight_b * out_b) / total, top + jnp.log2(total)


def finish(q_ref, blocks, acc_in, stat_in):
    state = load_state(acc_in, stat_in)
    above, keys, values = blocks
    pairs = [other_rows(above), (keys, values)]
    top, total, acc = absorb_blocks(state, q_ref[...], pairs)
    return acc / total, top + jnp.log2(total)


def far_kernel(q_ref, acc_in, stat_in, *refs):
    blocks, sent_ref = refs[:-1], refs[-1]
    out, lse = finish(q_ref, blocks, acc_in, stat_in)
    store_sent(sent_ref, out, narrow(lse))


def near_kernel(q_ref, acc_in, stat_in, *refs):
    blocks, (got_ref, out_ref, lines_ref, sent_ref) = refs[:-4], refs[-4:]
    out, lse = finish(q_ref, blocks, acc_in, stat_in)
    out, lse = merge(out, jnp.broadcast_to(lse, out.shape), *load_sent(got_ref))
    lines = narrow(lse[:, 0:1])
    out_ref[...] = out
    lines_ref[...] = lines
    store_sent(sent_ref, out, lines)


def last_merge_kernel(part, lengths_ref, out_ref, lines_ref, got_ref, attended_ref):
    tokens, width = attended_ref.shape
    rows = out_ref.shape[0]
    half = rows // 2
    got, got_lse = load_sent(got_ref)
    got = jnp.concatenate([got[half:], got[:half]], axis=0)
    got_lse = jnp.concatenate([got_lse[half:], got_lse[:half]], axis=0)
    out, _ = merge(out_ref[...], widen(lines_ref[...], rows), got, got_lse)
    row = lax.broadcasted_iota(jnp.int32, (tokens, LANES), 0)
    count = lengths_ref.shape[0]
    per = tokens // count
    token = (row % per) // SLAB * (PARTS * SLAB) + part * SLAB + row % SLAB
    valid = jnp.zeros((tokens, LANES), jnp.int32)
    for r in range(count):
        valid = jnp.where(row // per == r, lengths_ref[r], valid)
    live = token < valid
    for i in range(width // HEAD_SIZE):
        head = jnp.where(live, out[i * tokens : (i + 1) * tokens], 0.0)
        attended_ref[:, i * HEAD_SIZE : (i + 1) * HEAD_SIZE] = head.astype(BF16)


def project_kernel(w_ref, a_ref, b_ref, *refs):
    out_ref = refs[-1]
    devices, _, rows, width = out_ref.shape
    depth = w_ref.shape[1] // 4
    product = 0.0
    for i in range(4):
        ref, at = (a_ref, b_ref)[i % 2], i // 2 * depth
        weight = w_ref[:, i * depth : (i + 1) * depth]
        product = product + score_dot(ref[:, at : at + depth], weight)
    out_ref[:, 0] = product.reshape(devices, rows, width).astype(BF16)


def total_kernel(blocks, xh_ref, *refs):
    parts, out_ref = refs[:-1], refs[-1]
    half = out_ref.shape[1] // 2
    lines = []
    for ref in parts:
        count, rows, columns = ref.shape
        sums = ref[...].astype(F32).reshape(count // SLOTS, SLOTS, rows, columns).sum(0)
        piece = columns // blocks
        turned = []
        for rel in range(2):
            starts = range(rel * piece, columns, 2 * piece)
            pieces = [sums[q][:, at : at + piece] for at in starts for q in range(SLOTS)]
            turned.append(jnp.concatenate(pieces, axis=1))
        lines.append(turned)
    here = jnp.concatenate([line[0] for line in lines], axis=0).astype(BF16)
    there = jnp.concatenate([line[1] for line in lines], axis=0).astype(BF16)
    at_here = pl.multiple_of(xh_ref[0] * half, half)
    at_there = pl.multiple_of((1 - xh_ref[0]) * half, half)
    out_ref[:, pl.ds(at_here, half)] = here
    out_ref[:, pl.ds(at_there, half)] = there


def call(kernel, name, micros, order=(), in_specs=(), **options):
    def run(*operands):
        held = jnp.zeros((1,), jnp.int32)
        if order:
            held = after(held, *order)
        return pl.pallas_call(
            lambda held_ref, *refs: kernel(*refs),
            name=name,
            in_specs=[SMEM, *in_specs],
            cost_estimate=pl.CostEstimate(
                flops=int(micros * FLOPS_PER_MICRO), bytes_accessed=1, transcendentals=0
            ),
            compiler_params=pltpu.CompilerParams(vmem_limit_bytes=VMEM_LIMIT),
            **options,
        )(held, *operands)

    return run


def whole(array):
    return pl.BlockSpec(array.shape, lambda i: (0,) * array.ndim)


def rows_spec(tile, index=lambda i: i):
    return pl.BlockSpec((tile, HEAD_SIZE), lambda i: (index(i), 0))


def shapes_of(arrays):
    return [jax.ShapeDtypeStruct(a.shape, a.dtype) for a in arrays]


VMEM = pl.BlockSpec(memory_space=pltpu.VMEM)
SMEM = pl.BlockSpec(memory_space=pltpu.SMEM)


def first_own(q, resp_k, resp_v, block, order):
    tile = q.shape[0] // PARTS
    state = jax.ShapeDtypeStruct(q.shape, F32)
    return call(
        first_own_kernel,
        "attend_own",
        5,
        order,
        grid=(PARTS,),
        in_specs=[rows_spec(tile), whole(resp_k), whole(resp_v), whole(block)],
        out_specs=[rows_spec(tile)] * 2,
        out_shape=[state] * 2,
    )(q, resp_k, resp_v, block)


def first_all(q, block, near_block, own_state, tile, order):
    own_rows = q.shape[0] // (PARTS * SLOTS)
    state = jax.ShapeDtypeStruct(q.shape, F32)
    tiles = q.shape[0] // tile
    held = rows_spec(own_rows, lambda i: i * PARTS // tiles)
    return call(
        first_all_kernel,
        "attend_first",
        11,
        order,
        grid=(tiles,),
        in_specs=[rows_spec(tile), whole(block), whole(near_block), held, held],
        out_specs=[rows_spec(tile)] * 2,
        out_shape=[state] * 2,
    )(q, block, near_block, *own_state)


def attend_more(q, blocks, state, tile, order, start=0, rows=None):
    rows = rows or q.shape[0]
    count = len(blocks)
    at = start // tile
    moved = rows_spec(tile, lambda i: i + at)
    return call(
        functools.partial(middle_kernel, count),
        "attend_more",
        7 * count * rows // q.shape[0],
        order,
        grid=(rows // tile,),
        in_specs=[moved] + [whole(b) for b in blocks] + [moved] * 2,
        out_specs=[rows_spec(tile)] * 2,
        out_shape=[jax.ShapeDtypeStruct((rows, HEAD_SIZE), F32)] * 2,
    )(q, *blocks, *state)


def attend_far(q, blocks, state, part, rows, order):
    moved = rows_spec(rows, lambda i: 2 * part + 1)
    sent = jax.ShapeDtypeStruct((rows + 3 * STAT_ROWS, HEAD_SIZE), BF16)
    return call(
        far_kernel,
        "attend_far",
        2,
        order,
        grid=(1,),
        in_specs=[moved] * 3 + [whole(b) for b in blocks],
        out_specs=whole(sent),
        out_shape=sent,
    )(q, *state, *blocks)


def attend_near(q, blocks, state, got, part, rows, order):
    moved = rows_spec(rows, lambda i: 2 * part)
    out_shape = [
        jax.ShapeDtypeStruct((rows, HEAD_SIZE), F32),
        jax.ShapeDtypeStruct((STAT_ROWS, LANES), F32),
        jax.ShapeDtypeStruct(got.shape, BF16),
    ]
    return call(
        near_kernel,
        "attend_near",
        2,
        order,
        grid=(1,),
        in_specs=[moved] * 3 + [whole(b) for b in blocks] + [whole(got)],
        out_specs=[whole(s) for s in out_shape],
        out_shape=out_shape,
    )(q, *state, *blocks, got)


def last_merge(part, lengths, out, lines, got, tokens, order):
    attended = jax.ShapeDtypeStruct((tokens, out.shape[0] // tokens * HEAD_SIZE), BF16)
    return call(
        functools.partial(last_merge_kernel, part),
        "merge_last",
        1,
        order,
        grid=(1,),
        in_specs=[SMEM] + [whole(a) for a in (out, lines, got)],
        out_specs=whole(attended),
        out_shape=attended,
    )(lengths, out, lines, got)


def project(part, a, b, weight, before, tile=640):
    devices = a.shape[0] // SLAB
    columns, depth = weight.shape
    return call(
        project_kernel,
        "project",
        2,
        grid=(columns // tile,),
        in_specs=[pl.BlockSpec((tile, depth), lambda i: (i, 0)), whole(a), whole(b)]
        + [pl.BlockSpec(memory_space=pl.ANY)] * len(before),
        out_specs=pl.BlockSpec((devices, 1, SLAB, tile), lambda i: (0, part, 0, i)),
        out_shape=jax.ShapeDtypeStruct((devices, PARTS, SLAB, columns), BF16),
        input_output_aliases={4: 0} if before else {},
    )(weight, a, b, *before)


def add_up(xh, parts, width, blocks):
    rows = sum(part.shape[1] for part in parts)
    out = jax.ShapeDtypeStruct((rows, width), BF16)
    return call(
        functools.partial(total_kernel, blocks),
        "add_up",
        2,
        grid=(1,),
        in_specs=[SMEM] + [whole(p) for p in parts],
        out_specs=whole(out),
        out_shape=out,
    )(xh.reshape(1), *parts)


def pack_kernel(z_ref, y_ref, k_ref, v_ref, own_ref, sent_ref):
    groups, _, count, _ = sent_ref.shape
    here = pl.ds(pl.multiple_of(z_ref[0] * HEAD_SIZE, HEAD_SIZE), HEAD_SIZE)
    own_ref[0] = k_ref[:, here]
    own_ref[1] = v_ref[:, here]
    rows = pl.ds(pl.multiple_of(y_ref[0] * count, count), count)
    for group in range(groups):
        columns = slice(group * HEAD_SIZE, (group + 1) * HEAD_SIZE)
        sent_ref[group, 0] = k_ref[rows, columns]
        sent_ref[group, 1] = v_ref[rows, columns]


def pack(z, y, y_size, keys, values):
    groups = keys.shape[1] // HEAD_SIZE
    count = keys.shape[0]
    out_shape = [
        jax.ShapeDtypeStruct((2, count, HEAD_SIZE), BF16),
        jax.ShapeDtypeStruct((groups, 2, count // y_size, HEAD_SIZE), BF16),
    ]
    return call(
        pack_kernel,
        "pack_heads",
        2,
        grid=(1,),
        in_specs=[SMEM] * 2 + [whole(keys), whole(values)],
        out_specs=[whole(s) for s in out_shape],
        out_shape=out_shape,
    )(z.reshape(1), y.reshape(1), keys, values)


def unpack_kernel(z_ref, got_ref, out_ref):
    groups, _, count, _ = got_ref.shape
    for i in range(groups - 1):
        source = lax.rem(z_ref[0] + 1 + i, groups)
        out_ref[0, i * count : (i + 1) * count] = got_ref[source, 0]
        out_ref[1, i * count : (i + 1) * count] = got_ref[source, 1]


def unpack(z, got, order):
    groups, two, count, width = got.shape
    out = jax.ShapeDtypeStruct((two, (groups - 1) * count, width), BF16)
    return call(
        unpack_kernel,
        "unpack_heads",
        1,
        order,
        grid=(1,),
        in_specs=[SMEM, whole(got)],
        out_specs=whole(out),
        out_shape=out,
    )(z.reshape(1), got)


def after(array, *others):
    return lax.optimization_barrier((array, *others))[0]


def weight_of_core(out_weight, c):
    depth, width = out_weight.shape
    quarters = out_weight.T.reshape(2, 2, width // 4, depth)
    of_c = lax.dynamic_index_in_dim(quarters, c, 1, keepdims=False)
    sent = lax.dynamic_index_in_dim(quarters, 1 - c, 1, keepdims=False)
    return jnp.concatenate([of_c, lax.ppermute(sent, "c", SWAP)], axis=2)


def on_device(queries, keys, values, resp_keys, resp_values, lengths, out_weight):
    xh, y, z, xl, c = (lax.axis_index(a) for a in SUB_AXES)
    resp_count, resp_len, features = queries.shape
    tokens = resp_count * resp_len
    y_size = lax.axis_size("y")
    own_heads = features // HEAD_SIZE
    part_tokens = tokens // PARTS
    slot_rows = own_heads * part_tokens
    width = out_weight.shape[1]

    both = weight_of_core(out_weight, c)
    w_own = lax.dynamic_index_in_dim(both, xl, 0, keepdims=False)
    w_sent = lax.dynamic_index_in_dim(both, 1 - xl, 0, keepdims=False)
    w_x = lax.ppermute(w_sent, "xl", SWAP)
    w_h = lax.ppermute(w_own, "xh", SWAP)
    w_xh = lax.ppermute(w_sent, ("xh", "xl"), [(i, 3 - i) for i in range(4)])
    own_block, sent = pack(z, y, y_size, keys, values)
    got = lax.all_to_all(after(sent, both), "z", split_axis=0, concat_axis=0, tiled=True)

    q_own = after(queries, own_block).reshape(-1, PARTS, SLAB, own_heads, HEAD_SIZE)
    q_own = q_own.transpose(1, 3, 0, 2, 4).reshape(PARTS * slot_rows, HEAD_SIZE)
    q_every = lax.all_gather(q_own, ("xl", "c"), axis=0, tiled=False)

    up = [(i, (i + 1) % y_size) for i in range(y_size)]
    down = [(i, (i - 1) % y_size) for i in range(y_size)]
    head = z * HEAD_SIZE
    rk = lax.dynamic_slice_in_dim(resp_keys, head, HEAD_SIZE, 2)
    rv = lax.dynamic_slice_in_dim(resp_values, head, HEAD_SIZE, 2)
    state = first_own(q_own, rk, rv, own_block, ())
    near_y = unpack(z, after(got, state[0]), (w_x, w_h, w_xh))
    from_below = lax.ppermute(near_y, "y", up)
    from_above = lax.ppermute(near_y, "y", down)
    here = jnp.concatenate([w_own, w_x], axis=1)
    there = jnp.concatenate([w_h, w_xh], axis=1)
    weight = lax.all_gather(jnp.concatenate([here, there], axis=0), "y", axis=0, tiled=True)

    q_every = after(q_every, state[0])
    mine = 2 * xl + c
    slots = [q_own] + [
        lax.dynamic_index_in_dim(q_every, mine ^ i, 0, keepdims=False) for i in (2, 1, 3)
    ]
    slots = [q.reshape(PARTS, 1, slot_rows, HEAD_SIZE) for q in slots]
    q_all = jnp.concatenate(slots, axis=1).reshape(-1, HEAD_SIZE)
    state = first_all(q_all, own_block, near_y, state, 1024, ())
    far_k = lax.ppermute(after(from_below, state[0])[0], "y", up)
    far_v = lax.ppermute(after(from_above, state[0])[1], "y", down)
    state = attend_more(q_all, [near_y, from_below, from_above], state, 1024, ())
    half = 2 * slot_rows
    blocks = [from_above, far_k, far_v]
    far = []
    for part in range(PARTS):
        order = (far[-1],) if far else ()
        far.append(attend_far(q_all, blocks, state, part, half, order))
    far_c = [lax.ppermute(f, "c", SWAP) for f in far]
    near, near_x = [], []
    for part in range(PARTS):
        order = (near[-1][0],) if near else (far[-1],)
        out, lines, sent = attend_near(q_all, blocks, state, far_c[part], part, half, order)
        near.append((out, lines))
        near_x.append(lax.ppermute(sent, "xl", SWAP))
    partial = ()
    for part in range(PARTS):
        order = (near[-1][0], *partial)
        attended = last_merge(part, lengths, *near[part], near_x[part], part_tokens, order)
        attended_c = lax.ppermute(attended, "c", SWAP)
        partial = (project(part, attended, attended_c, weight, partial),)
    partial = partial[0]
    partial = partial.reshape(partial.shape[0], PARTS * SLAB, partial.shape[-1])
    received = lax.all_to_all(partial, PREFIX, split_axis=0, concat_axis=0, tiled=True)
    blocks = 2 * y_size
    return add_up(xh, [received], width * blocks, blocks)


def solution(mesh):
    shape = (2, mesh.shape["batch"] // 2, mesh.shape["prefix"] // 4, 2, 2)
    fine = Mesh(mesh.devices.reshape(shape), SUB_AXES)
    batch = ("xh", "y")
    placed = (
        P(batch, None, PREFIX),
        P(PREFIX, None),
        P(PREFIX, None),
        P(batch, None, None),
        P(batch, None, None),
        P(batch),
        P(PREFIX, batch),
    )
    return jax.shard_map(
        on_device,
        mesh=fine,
        in_specs=placed,
        out_specs=P(batch + PREFIX, None),
        check_vma=False,
    )
```
